32 devices in a mesh: groups: 2 (over y), tensor: 4 (over z), query: 2 (over x), dp: 2 (over core).
Axes of the slice: x: 2, y: 2, z: 4, core: 2. Of those that a mesh axis runs over, the one named last changes fastest.
Arguments:
- features: bfloat16 [2048, 8192], P(('groups', 'dp'), 'query'), parts along dimension 0, may hold values from -6 to 6
- up_weight: bfloat16 [8192, 28672], P(('query', 'dp'), 'tensor'), may hold values from -0.09375 to 0.09375
- out_grad: bfloat16 [2048, 28672], P(('groups', 'dp'), 'tensor'), parts along dimension 0, may hold values from -6 to 6
- left_factors: bfloat16 [16, 32, 28672], P('query', None, 'tensor'), may hold values from -0.03125 to 0.03125
- right_factors: bfloat16 [16, 32, 8192], P('query', None, 'tensor'), may hold values from -0.0625 to 0.0625
- token_ids: int32 [2048], P(('groups', 'dp')), parts along dimension 0, may hold values from 0 to 15, never falling along the last dimension, each value on 1 to 128 neighbouring positions
- query_ids: int32 [2, 8], P('query'), may hold values from 0 to 7, each once within a row
Outputs:
- input_grad: bfloat16 [2048, 8192], P(('groups', 'dp'), ('query', 'tensor')), parts along dimension 0
- scores: float32 [32, 16], P('groups', 'query'), parts along dimension 0
The draws below stay inside these ranges and needn't reach their ends.
There are 2 independent parts, one for each index of `groups`. The reference program is written for one: setup_inputs(seed, part) draws one part's arguments, and reference() takes and returns one part's arrays. A program takes and returns all parts, laid end to end along the dimension named above; an argument that names none is the same for every part. Nothing has to cross between parts.
Inputs may be any that keep to these rules, and one draw needn't show every extreme that they name: token_ids never fall along the tokens; every example has at least one token. `query_ids`: each row is a permutation of the numbers below 8.
All inputs are finite; a program needn't handle non-finite values.
Results may differ from the reference program's by a relative error of at most 0.0049.
Values may be sent and summed in bfloat16 or wider, within the bound.
No kernel may reach another device: no remote copies, remote signals or barrier semaphores. Data moves between devices by JAX's collectives and lax.ppermute only.
A program may use at most 192 MiB of HBM per device.

```python
import math
import jax
import jax.numpy as jnp
import numpy as np
from jax import lax

D = 8192
FF = 28672
R = 32
QPD = 8
EXAMPLES = 16
QSHARDS = 2
QUERIES = 16
TOKENS = 1024


def with_spikes(array, stream_key, source, target, parts, factor):
    owner, partner = [(jnp.arange(array.shape[position]) // (array.shape[position] // parts)).reshape([-1 if axis == position else 1 for axis in range(array.ndim)]) for position in (source, target)]
    chosen = jax.random.permutation(stream_key, parts)[partner]
    strong = (owner == chosen) | (owner == (partner + parts // 2) % parts)
    return jnp.where(strong, factor * array, array)


def levels(own_key, dims, cuts, least, top_value):
    def one(position, blocks):
        heights = jax.random.uniform(jax.random.fold_in(jax.random.fold_in(own_key, 6), position), (blocks,), jnp.float32, least / len(cuts), top_value / len(cuts))
        return jnp.repeat(jnp.exp(heights), dims[position] // blocks).reshape((-1,) + (1,) * (len(dims) - position - 1))

    factor_of = one(*cuts[0])
    for cut in cuts[1:]:
        factor_of = factor_of * one(*cut)
    return factor_of


def split_up(number_of, total, limit, skew):
    loads = [(1 << 20) // math.isqrt(standing ** skew) + 1 for standing in range(2, number_of + 1)]
    surplus, given = total - limit - (number_of - 1), [1] * (number_of - 1)
    while surplus > 0:
        movable = [i for i in range(number_of - 1) if given[i] < limit]
        whole, budget = sum([loads[i] for i in movable]), surplus
        for i in movable:
            addition = min(limit - given[i], max(1, budget * loads[i] // whole), surplus)
            given[i] = given[i] + addition
            surplus = surplus - addition
    return np.array([limit] + given)


def uneven(stream_key, amount, total, reach, lean):
    if amount == 2:
        one = jax.random.randint(stream_key, (), max(1, total - reach), min(reach, total - 1) + 1)
        return jnp.stack([one, total - one])
    sizes = jnp.asarray(split_up(amount, total, reach, lean), jnp.int32)
    pairs = (amount - 1) // 2
    giver, receiver = sizes[1:1 + 2 * pairs:2], sizes[2:2 + 2 * pairs:2]
    room = jnp.minimum(giver - 1, reach - receiver)
    moved = jax.random.randint(jax.random.fold_in(stream_key, 1), (pairs,), 0, 1 << 20) % (room + 1)
    sizes = sizes.at[1:1 + 2 * pairs:2].set(giver - moved).at[2:2 + 2 * pairs:2].set(receiver + moved)
    return sizes[jax.random.permutation(jax.random.fold_in(stream_key, 2), amount)]


def normal_values(own_key, shape, spread, reach, cuts=(), held_as=jnp.bfloat16):
    values = jax.random.normal(own_key, shape, jnp.float32) * spread
    if len(cuts) > 0:
        values = levels(own_key, shape, cuts, -0.22, 0.18) * values
    return jnp.clip(values, min=-reach, max=reach).astype(held_as)


def noise_with(own_key, dims, deviation, most, shards, heavy, kind=jnp.bfloat16):
    result = deviation * jax.random.normal(own_key, dims, jnp.float32)
    if shards:
        result = result * levels(own_key, dims, shards, -0.22, 0.18)
    return jnp.clip(with_spikes(result, jax.random.fold_in(own_key, 3), *heavy), -most, most).astype(kind)


def setup_inputs(seed: int = 0, part: int = 0) -> dict:
    arg_keys = jax.random.split(jax.random.key(seed), 8)
    part_keys = jax.random.split(jax.random.fold_in(arg_keys[7], part), 8)
    features = normal_values(part_keys[0], (TOKENS, D), 1.0, 6.0, ((0, 2), (1, 2)))
    up_weight = noise_with(arg_keys[1], (D, FF), D ** -0.5, 0.09375, ((0, 4), (1, 4)), (1, 0, 4, 2.0))
    out_grad = normal_values(part_keys[2], (TOKENS, FF), 1.0, 6.0, ((0, 2), (1, 4)))
    left_factors = normal_values(arg_keys[3], (QUERIES, R, FF), FF ** -0.5, 0.03125, ((0, 2), (2, 4)))
    right_factors = normal_values(arg_keys[4], (QUERIES, R, D), D ** -0.5, 0.0625, ((0, 2), (2, 4)))
    token_ids = jnp.searchsorted(jnp.cumsum(uneven(part_keys[5], EXAMPLES, TOKENS, 2 * TOKENS // EXAMPLES, 1)), jnp.arange(TOKENS), side="right").astype(jnp.int32)
    query_ids = jax.vmap(lambda own: jax.random.permutation(own, QPD))(jax.random.split(arg_keys[6], QSHARDS)).reshape((QSHARDS, QPD)).astype(jnp.int32)
    return {"features": features, "up_weight": up_weight, "out_grad": out_grad, "left_factors": left_factors, "right_factors": right_factors, "token_ids": token_ids, "query_ids": query_ids}


def reference(features, up_weight, out_grad, left_factors, right_factors, token_ids, query_ids):
    preact = jnp.dot(features, up_weight, preferred_element_type=jnp.float32)
    sigmoid_value = jax.nn.sigmoid(preact)
    grad_rows = (out_grad.astype(jnp.float32) * sigmoid_value * (1.0 + preact * (1.0 - sigmoid_value))).astype(jnp.bfloat16)
    input_grad = lax.dot_general(grad_rows, up_weight, (((1,), (1,)), ((), ())), preferred_element_type=jnp.float32).astype(jnp.bfloat16)
    left_proj = lax.dot_general(grad_rows, left_factors.reshape(QUERIES * R, FF), (((1,), (1,)), ((), ())), preferred_element_type=jnp.float32)
    right_proj = lax.dot_general(features, right_factors.reshape(QUERIES * R, D), (((1,), (1,)), ((), ())), preferred_element_type=jnp.float32)
    per_token = (left_proj * right_proj).reshape(TOKENS, QUERIES, R).sum(axis=-1)
    membership = (token_ids[None, :] == jnp.arange(EXAMPLES, dtype=jnp.int32)[:, None]).astype(jnp.float32)
    summed = jnp.dot(membership, per_token, precision=lax.Precision.HIGHEST, preferred_element_type=jnp.float32) / R
    positions = (jnp.arange(QSHARDS, dtype=jnp.int32)[:, None] * QPD + query_ids).reshape(-1).astype(jnp.int32)
    scores = jnp.take(summed, positions, axis=1)
    return input_grad, scores
```

```python
import jax
import jax.numpy as jnp
from jax import lax
from jax.experimental import pallas as pl
from jax.experimental.pallas import tpu as pltpu
from jax.sharding import PartitionSpec as P

EXAMPLES = 16
LANES = 128
TOKEN_SHARES = (3, 2, 2, 1)
HEAD_SHARES = (1, 2, 4)
REST_SHARES = (4, 3)
VMEM_BYTES = 48 << 20
F32, BF16 = jnp.float32, jnp.bfloat16


def silu_slope(preact, grad_part):
    sigmoid_value = jax.nn.sigmoid(preact)
    return (
        grad_part.astype(jnp.float32) * sigmoid_value * (1.0 + preact * (1.0 - sigmoid_value))
    ).astype(jnp.bfloat16)


def contract_last(left_rows, right_rows):
    return lax.dot_general(
        left_rows, right_rows, (((1,), (1,)), ((), ())), preferred_element_type=jnp.float32
    )


def cuts(total, unit, shares):
    whole, marks, seen = sum(shares), [0], 0
    for share in shares:
        seen += share
        mark = total * seen // whole // unit * unit if seen < whole else total
        if mark > marks[-1]:
            marks.append(mark)
    return list(zip(marks[:-1], marks[1:]))


def column_choice(query_ids, query_count, rank_count):
    owner = jnp.arange(query_count * rank_count, dtype=jnp.int32) // rank_count
    return (owner[:, None] == query_ids[0][None, :]).astype(jnp.float32)


def exact_dot(a, b):
    return jnp.dot(a, b, precision=lax.Precision.HIGHEST, preferred_element_type=jnp.float32)


def right_projection(features, right_rows):
    block_width = right_rows.shape[1]
    tensor_size = lax.axis_size("tensor")
    fold = tensor_size // 2
    tensor_index, query_index = lax.axis_index("tensor"), lax.axis_index("query")
    owns = tensor_index // fold == query_index
    there = [(2 * t + 1 - t // fold, 2 * t + t // fold) for t in range(tensor_size)]
    back = [(b, a) for a, b in there]
    half = right_rows.shape[0] // 2
    piece = lax.dynamic_slice_in_dim(right_rows, lax.axis_index("dp") * half, half, 0)
    piece = lax.ppermute(piece, ("tensor", "query"), there)
    other_rows = lax.all_gather(piece, "dp", axis=0, tiled=True)
    block = lax.dynamic_slice_in_dim(features, tensor_index % fold * block_width, block_width, 1)
    for_other = contract_last(block, other_rows).astype(jnp.bfloat16)
    received = lax.ppermute(for_other, ("tensor", "query"), back)
    part = jnp.where(owns, contract_last(block, right_rows), received.astype(jnp.float32))
    return lax.psum(part, "tensor")


def tile_of(width, limit):
    return max(t for t in range(LANES, limit + 1, LANES) if width % t == 0)


def ordered(body, after, in_specs, out_specs, out_shape, **kwargs):
    def kernel(mark, *refs):
        inputs, rest = refs[: len(in_specs)], refs[len(in_specs) :]
        outputs, own_mark, scratch = (
            rest[: len(out_specs)],
            rest[len(out_specs)],
            rest[len(out_specs) + 1 :],
        )
        own_mark[...] = jnp.zeros_like(own_mark)
        body(inputs, outputs, scratch)

    mark_spec = pl.BlockSpec((8, LANES), lambda *ids: (0, 0))

    def call(*operands):
        return pl.pallas_call(
            kernel,
            in_specs=[pl.BlockSpec(memory_space=pl.ANY)] + list(in_specs),
            out_specs=list(out_specs) + [mark_spec],
            out_shape=list(out_shape) + [jax.ShapeDtypeStruct((8, LANES), F32)],
            compiler_params=pltpu.CompilerParams(vmem_limit_bytes=VMEM_BYTES),
            cost_estimate=pl.CostEstimate(flops=1, bytes_accessed=1, transcendentals=0),
            **kwargs,
        )(after, *operands)

    return call


def forward(rows, up_weight, span, spans_of_tokens, after):
    low, high = span
    depth = up_weight.shape[0]
    tile = tile_of(_gcd(high - low, low), 1024)
    count = rows.shape[0] // 2
    first = spans_of_tokens[0][0]

    def body(inputs, outputs, scratch):
        product = jnp.dot(inputs[0][...], inputs[1][...], preferred_element_type=F32)
        for n, (a, b) in enumerate(spans_of_tokens):
            outputs[2 * n][...] = product[a - first : b - first]
            outputs[2 * n + 1][...] = product[count + a - first : count + b - first].astype(BF16)

    out_specs, out_shape = [], []
    for a, b in spans_of_tokens:
        for kind in (F32, BF16):
            out_specs.append(pl.BlockSpec((b - a, tile), lambda i: (0, i)))
            out_shape.append(jax.ShapeDtypeStruct((b - a, high - low), kind))
    *results, mark = ordered(
        body,
        after,
        [
            pl.BlockSpec(rows.shape, lambda i: (0, 0)),
            pl.BlockSpec((depth, tile), lambda i: (0, low // tile + i)),
        ],
        out_specs,
        out_shape,
        grid=((high - low) // tile,),
    )(rows, up_weight)
    return list(zip(results[0::2], results[1::2])), mark


def _gcd(x, y):
    while y:
        x, y = y, x % y
    return x


def elementwise(slope, add, after):
    widths = ([slope[0].shape[1]] if slope else []) + ([add[0].shape[1]] if add else [])
    steps = max(n for n in (1, 2, 4) if all(w % (n * LANES) == 0 for w in widths))

    def spec(array):
        return pl.BlockSpec((array.shape[0], array.shape[1] // steps), lambda i: (0, i))

    in_specs, operands, out_specs, out_shape = [], [], [], []
    if slope:
        mine, theirs, out_grad, (low, high), (a, b) = slope
        width = (b - a) // steps
        in_specs += [
            spec(mine),
            spec(theirs),
            pl.BlockSpec(
                (pl.Element(high - low), pl.Element(width)),
                lambda i: (low, pl.multiple_of(a + i * width, LANES)),
            ),
        ]
        operands += [mine, theirs, out_grad]
        out_specs.append(spec(mine))
        out_shape.append(jax.ShapeDtypeStruct(mine.shape, BF16))
    if add:
        in_specs += [spec(add[0]), spec(add[1])]
        operands += add
        out_specs.append(spec(add[0]))
        out_shape.append(jax.ShapeDtypeStruct(add[0].shape, BF16))

    def body(inputs, outputs, scratch):
        if slope:
            preact = inputs[0][...].astype(F32) + inputs[1][...].astype(F32)
            sigmoid_value = 0.5 * jnp.tanh(0.5 * preact) + 0.5
            outputs[0][...] = (
                inputs[2][...].astype(F32)
                * sigmoid_value
                * (1.0 + preact * (1.0 - sigmoid_value))
            ).astype(BF16)
        if add:
            outputs[-1][...] = (inputs[-2][...] + inputs[-1][...].astype(F32)).astype(BF16)

    *results, mark = ordered(body, after, in_specs, out_specs, out_shape, grid=(steps,))(*operands)
    return results, mark


def backward(own_rows, other_rows, up_weight, left_rows, span, total, place, blocks, last, after):
    low, high = span
    depth, count = up_weight.shape[0], own_rows.shape[0]
    width = depth // blocks
    pieces = 2 * blocks
    tile = tile_of(_gcd(high - low, low), 1024)
    steps = (high - low) // tile

    def body(inputs, outputs, scratch):
        step = pl.program_id(0)
        place_ref, own, other, weight, left = inputs[:5]
        sums, left_sums = scratch if last else outputs

        @pl.when(step == 0)
        def _():
            if total is None:
                sums[...] = jnp.zeros_like(sums)
                left_sums[...] = jnp.zeros_like(left_sums)
            else:
                sums[...] = inputs[5][...]
                left_sums[...] = inputs[6][...]

        both = jnp.concatenate([own[...], other[...]], axis=0)
        for block in range(blocks):
            product = contract_last(both, weight[block * width : (block + 1) * width, :])
            sums[2 * block] += product[:count]
            sums[2 * block + 1] += product[count:]
        left_sums[...] += contract_last(own[...], left[...])
        if last:

            @pl.when(step == steps - 1)
            def _():
                for n in range(pieces):
                    outputs[n][...] = sums[lax.rem(place_ref[0] + n, pieces)].astype(BF16)
                outputs[pieces][...] = left_sums[...]

    tokens_spec = pl.BlockSpec((count, tile), lambda i: (0, i))
    sums_shape, left_shape = (pieces, count, width), (count, left_rows.shape[0])
    sums_spec = pl.BlockSpec(sums_shape, lambda i: (0, 0, 0))
    left_spec = pl.BlockSpec(left_shape, lambda i: (0, 0))
    in_specs = [
        pl.BlockSpec(memory_space=pltpu.SMEM),
        tokens_spec,
        tokens_spec,
        pl.BlockSpec((depth, tile), lambda i: (0, low // tile + i)),
        pl.BlockSpec((left_rows.shape[0], tile), lambda i: (0, low // tile + i)),
    ]
    operands = [place, own_rows, other_rows, up_weight, left_rows]
    if total is not None:
        in_specs += [sums_spec, left_spec]
        operands += total
    if last:
        out_specs = [pl.BlockSpec((count, width), lambda i: (0, 0))] * pieces + [left_spec]
        out_shape = [jax.ShapeDtypeStruct((count, width), BF16)] * pieces
        out_shape.append(jax.ShapeDtypeStruct(left_shape, F32))
        scratch = [pltpu.VMEM(sums_shape, F32), pltpu.VMEM(left_shape, F32)]
    else:
        out_specs = [sums_spec, left_spec]
        out_shape = [jax.ShapeDtypeStruct(sums_shape, F32), jax.ShapeDtypeStruct(left_shape, F32)]
        scratch = []
    *results, mark = ordered(
        body, after, in_specs, out_specs, out_shape, grid=(steps,), scratch_shapes=scratch
    )(*operands)
    return results, mark


def exchange(messages, blocks):
    tensor_size = lax.axis_size("tensor")
    pieces = 2 * blocks
    total = None
    for n, message in enumerate(messages):
        pairs = []
        for t in range(tensor_size):
            for c in range(2):
                target = (t + n) % pieces
                pairs.append((2 * t + c, 2 * (blocks * c + target // 2) + (c ^ (target % 2))))
        arrived = lax.ppermute(message, ("tensor", "dp"), pairs).astype(F32)
        total = arrived if total is None else total + arrived
    return total.astype(BF16)


def paired(features, up_weight, out_grad, left_factors, right_factors, token_ids, query_ids):
    query_count, rank_count = left_factors.shape[:2]
    left_rows = left_factors.reshape(query_count * rank_count, left_factors.shape[2])
    right_rows = right_factors.reshape(query_count * rank_count, right_factors.shape[2])
    token_count, hidden = out_grad.shape
    depth = up_weight.shape[0]
    blocks = lax.axis_size("tensor") // 2
    core = lax.axis_index("dp")
    swap = [(0, 1), (1, 0)]
    place = lax.rem(lax.axis_index("tensor"), 2 * blocks).astype(jnp.int32).reshape(1)

    tokens = cuts(token_count, 16, TOKEN_SHARES)
    groups = [(tokens[:1], cuts(hidden, LANES, HEAD_SHARES)), (tokens[1:], cuts(hidden, LANES, REST_SHARES))]

    stacked = []
    for token_spans, _ in groups:
        low, high = token_spans[0][0], token_spans[-1][1]
        away = lax.dynamic_slice(features, (low, (1 - core) * depth), (high - low, depth))
        here = lax.dynamic_slice(features, (low, core * depth), (high - low, depth))
        stacked.append(jnp.concatenate([here, lax.ppermute(away, "dp", swap)], axis=0))
    right_sum = right_projection(features, right_rows)

    mark = jnp.zeros((8, LANES), F32)
    adds, pieces = {}, []
    for g, (token_spans, spans) in enumerate(groups):
        for t in token_spans:
            for s in spans:
                pieces.append((g, t, s, s == spans[-1]))

    def run_forward(g, span, mark):
        token_spans = groups[g][0]
        results, mark = forward(stacked[g], up_weight, span, token_spans, mark)
        for t, (own, send) in zip(token_spans, results):
            adds[t, span] = (own, lax.ppermute(send, "dp", swap))
        return mark

    def add_of(k):
        return adds[pieces[k][1], pieces[k][2]]

    mine, theirs, rows, totals, sums, lefts = {}, {}, {}, {}, {}, {}

    def send(k, half):
        mine[k] = half
        theirs[k] = lax.ppermute(half, "query", swap)

    def run_step(k, ahead, mark):
        slope = add = None
        if k is not None:
            slope = (mine[k], theirs[k], out_grad, pieces[k][1], pieces[k][2])
        if ahead is not None and ahead < len(pieces):
            add = add_of(ahead)
        results, mark = elementwise(slope, add, mark)
        if k is not None:
            rows[k] = (results[0], lax.ppermute(results[0], "dp", swap))
        if add is not None:
            send(ahead, results[-1])
        return mark

    def run_backward(k, mark):
        g, t, span, last = pieces[k]
        results, mark = backward(
            *rows[k], up_weight, left_rows, span, totals.get(t), place, blocks, last, mark
        )
        if last:
            sums[t], lefts[t] = exchange(results[:-1], blocks), results[-1]
        else:
            totals[t] = results
        return mark

    head, rest = groups[0][1], groups[1][1]
    mark = run_forward(0, head[0], mark)
    mark = run_step(None, 0, mark)
    mark = run_forward(0, head[1], mark)
    mark = run_step(None, 1, mark)
    mark = run_forward(0, head[2], mark)
    mark = run_step(0, 2, mark)
    mark = run_forward(1, rest[0], mark)
    mark = run_step(1, 3, mark)
    mark = run_backward(0, mark)
    mark = run_forward(1, rest[1], mark)
    mark = run_backward(1, mark)
    for k in range(2, len(pieces)):
        mark = run_step(k, k + 2, mark)
        mark = run_backward(k, mark)

    weighted = 0.0
    for low, high in tokens:
        membership = (
            token_ids[None, low:high] == jnp.arange(EXAMPLES, dtype=jnp.int32)[:, None]
        ).astype(F32)
        weighted = weighted + exact_dot(membership, lefts[low, high] * right_sum[low:high])
    choice = column_choice(query_ids, query_count, rank_count)
    scores = lax.psum(exact_dot(weighted, choice) / rank_count, ("tensor", "dp"))
    return jnp.concatenate([sums[t] for t in tokens], axis=0), scores


def broadcast(value, axis, source):
    kept = jnp.where(lax.axis_index(axis) == source, value, 0).astype(value.dtype)
    return lax.psum(kept, axis)


def general(features, up_weight, out_grad, left_factors, right_factors, token_ids, query_ids):
    query_count, rank_count = left_factors.shape[:2]
    local_rows = lax.all_gather(up_weight, "dp", axis=0, tiled=True)
    preact_part = jnp.dot(features, local_rows, preferred_element_type=jnp.float32)
    preact_share = lax.psum_scatter(preact_part, "query", scatter_dimension=0, tiled=True)
    share_rows = preact_share.shape[0]
    own_grad = lax.dynamic_slice_in_dim(
        out_grad, lax.axis_index("query") * share_rows, share_rows, 0
    )
    grad_rows = lax.all_gather(silu_slope(preact_share, own_grad), "query", axis=0, tiled=True)
    input_part = contract_last(grad_rows, local_rows)
    input_grad = lax.psum_scatter(input_part, "tensor", scatter_dimension=1, tiled=True).astype(
        jnp.bfloat16
    )
    fold_ratio = lax.axis_size("tensor") // lax.axis_size("query")
    tensor_index = lax.axis_index("tensor")
    block_width = right_factors.shape[2]
    feature_piece = lax.dynamic_slice_in_dim(
        features, tensor_index % fold_ratio * block_width, block_width, 1
    )
    feature_block = broadcast(feature_piece, "query", tensor_index // fold_ratio)
    left_proj = contract_last(
        grad_rows, left_factors.reshape(query_count * rank_count, left_factors.shape[2])
    )
    right_proj = contract_last(
        feature_block, right_factors.reshape(query_count * rank_count, block_width)
    )
    left_sum, right_sum = lax.psum((left_proj, right_proj), "tensor")
    membership = (token_ids[None, :] == jnp.arange(EXAMPLES, dtype=jnp.int32)[:, None]).astype(
        jnp.float32
    )
    weighted = exact_dot(membership, left_sum * right_sum)
    choice = column_choice(query_ids, query_count, rank_count)
    scores = lax.psum(exact_dot(weighted, choice) / rank_count, "dp")
    return (input_grad, scores)


def solution(mesh):
    size = mesh.shape
    is_paired = size["query"] == 2 and size["dp"] == 2 and size["tensor"] % 2 == 0
    return jax.shard_map(
        paired if is_paired else general,
        mesh=mesh,
        in_specs=(
            P(("groups", "dp"), "query"),
            P(("query", "dp"), "tensor"),
            P(("groups", "dp"), "tensor"),
            P("query", None, "tensor"),
            P("query", None, "tensor"),
            P(("groups", "dp")),
            P("query", None),
        ),
        out_specs=(P(("groups", "dp"), ("query", "tensor")), P("groups", "query")),
        check_vma=False,
    )
```

```python
import jax
import jax.numpy as jnp
from jax import lax
from jax.experimental import pallas as pl
from jax.experimental.pallas import tpu as pltpu
from jax.sharding import PartitionSpec as P

EXAMPLES = 16
LANES = 128
TOKEN_SHARES = (3, 3, 2)
HEAD_SHARES = (3, 4)
REST_SHARES = (4, 3)
FORWARD_MESSAGES = (3, 3, 1)
SLOPE_MESSAGES = 2
VMEM_BYTES = 36 << 20
F32, BF16 = jnp.float32, jnp.bfloat16


def silu_slope(preact, grad_part):
    sigmoid_value = jax.nn.sigmoid(preact)
    return (
        grad_part.astype(jnp.float32) * sigmoid_value * (1.0 + preact * (1.0 - sigmoid_value))
    ).astype(jnp.bfloat16)


def contract_last(left_rows, right_rows):
    return lax.dot_general(
        left_rows, right_rows, (((1,), (1,)), ((), ())), preferred_element_type=jnp.float32
    )


def cuts(total, unit, shares):
    whole, marks, seen = sum(shares), [0], 0
    for share in shares:
        seen += share
        mark = total * seen // whole // unit * unit if seen < whole else total
        if mark > marks[-1]:
            marks.append(mark)
    return list(zip(marks[:-1], marks[1:]))


def column_choice(query_ids, query_count, rank_count):
    owner = jnp.arange(query_count * rank_count, dtype=jnp.int32) // rank_count
    return (owner[:, None] == query_ids[0][None, :]).astype(jnp.float32)


def exact_dot(a, b):
    return jnp.dot(a, b, precision=lax.Precision.HIGHEST, preferred_element_type=jnp.float32)


def right_pairs(tensor_size):
    fold = tensor_size // 2
    return [(2 * t + 1 - t // fold, 2 * t + t // fold) for t in range(tensor_size)]


def right_send(right_rows):
    half = right_rows.shape[0] // 2
    piece = lax.dynamic_slice_in_dim(right_rows, lax.axis_index("dp") * half, half, 0)
    return lax.ppermute(piece, ("tensor", "query"), right_pairs(lax.axis_size("tensor")))


def right_products(features, right_rows, here, there, where, after):
    rows, depth = right_rows.shape
    half = rows // 2
    count = features.shape[0]

    def body(scalar_ref, inputs, outputs, scratch):
        block = inputs[0][...]
        outputs[0][...] = contract_last(block, inputs[1][...])
        first, second = contract_last(block, inputs[2][...]), contract_last(block, inputs[3][...])
        is_first = scalar_ref[0] == 0
        outputs[1][:, :half] = jnp.where(is_first, first, second).astype(BF16)
        outputs[1][:, half:] = jnp.where(is_first, second, first).astype(BF16)

    whole = pl.BlockSpec((count, rows), lambda i, *_: (0, 0))
    own, for_other, mark = ordered(
        "right",
        body,
        after,
        [
            pl.BlockSpec(
                (pl.Element(count), pl.Element(depth)),
                lambda i, where_ref: (0, pl.multiple_of(where_ref[1], LANES)),
            ),
            pl.BlockSpec((rows, depth), lambda i, *_: (0, 0)),
            pl.BlockSpec((half, depth), lambda i, *_: (0, 0)),
            pl.BlockSpec((half, depth), lambda i, *_: (0, 0)),
        ],
        [whole, whole],
        [jax.ShapeDtypeStruct((count, rows), F32), jax.ShapeDtypeStruct((count, rows), BF16)],
        scalars=where,
    )(features, right_rows, here, there)
    return own, for_other, mark


def right_choice(own, received, owns, after):
    def body(scalar_ref, inputs, outputs, scratch):
        outputs[0][...] = jnp.where(
            scalar_ref[0] == 1, inputs[0][...], inputs[1][...].astype(F32)
        ).astype(BF16)

    whole = pl.BlockSpec(own.shape, lambda i, *_: (0, 0))
    return ordered(
        "right_choice",
        body,
        after,
        [whole, whole],
        [whole],
        [jax.ShapeDtypeStruct(own.shape, BF16)],
        scalars=owns,
    )(own, received)


def tile_of(width, limit):
    return max(t for t in range(LANES, limit + 1, LANES) if width % t == 0)


def ordered(name, body, after, in_specs, out_specs, out_shape, grid=(1,), scratch_shapes=(), scalars=None, vmem=VMEM_BYTES):
    def kernel(scalar_ref, *refs):
        refs = refs[len(after) :]
        inputs, rest = refs[: len(in_specs)], refs[len(in_specs) :]
        outputs, own_mark, scratch = (
            rest[: len(out_specs)],
            rest[len(out_specs)],
            rest[len(out_specs) + 1 :],
        )
        own_mark[...] = jnp.zeros_like(own_mark)
        body(scalar_ref, inputs, outputs, scratch)

    mark_spec = pl.BlockSpec((8, LANES), lambda *ids: (0, 0))

    if scalars is None:
        scalars = jnp.zeros((1,), jnp.int32)

    def call(*operands):
        return pl.pallas_call(
            kernel,
            grid_spec=pltpu.PrefetchScalarGridSpec(
                num_scalar_prefetch=1,
                grid=grid,
                in_specs=[pl.BlockSpec(memory_space=pl.ANY)] * len(after) + list(in_specs),
                out_specs=list(out_specs) + [mark_spec],
                scratch_shapes=list(scratch_shapes),
            ),
            out_shape=list(out_shape) + [jax.ShapeDtypeStruct((8, LANES), F32)],
            compiler_params=pltpu.CompilerParams(vmem_limit_bytes=vmem),
            cost_estimate=pl.CostEstimate(flops=1, bytes_accessed=1, transcendentals=0),
            name=name,
        )(scalars, *after, *operands)

    return call


def half_of(features, tokens, depth, core, after):
    low, high = tokens

    def body(scalar_ref, inputs, outputs, scratch):
        outputs[0][...] = inputs[0][...]

    return ordered(
        "half",
        body,
        after,
        [
            pl.BlockSpec(
                (pl.Element(high - low), pl.Element(depth)),
                lambda i, core_ref: (low, pl.multiple_of((1 - core_ref[0]) * depth, LANES)),
            )
        ],
        [pl.BlockSpec((high - low, depth), lambda i, *_: (0, 0))],
        [jax.ShapeDtypeStruct((high - low, depth), features.dtype)],
        scalars=core,
    )(features)


def add_right(own, received, after):
    def body(scalar_ref, inputs, outputs, scratch):
        total = inputs[0][...].astype(F32) + inputs[1][...].astype(F32)
        outputs[0][...] = total
        outputs[1][...] = total.astype(BF16)

    whole = pl.BlockSpec(own.shape, lambda i, *_: (0, 0))
    total, message, mark = ordered(
        "add_right",
        body,
        after,
        [whole, whole],
        [whole, whole],
        [jax.ShapeDtypeStruct(own.shape, F32), jax.ShapeDtypeStruct(own.shape, BF16)],
    )(own, received)
    return total, message, mark


def in_messages(steps, tile, number):
    marks = cuts(steps * tile, LANES, (1,) * number)
    where = []
    for step in range(steps):
        parts = []
        for message, (low, high) in enumerate(marks):
            begin, end = max(low, step * tile), min(high, (step + 1) * tile)
            if begin < end:
                parts.append((message, begin - low, begin - step * tile, end - begin))
        where.append(parts)
    return where, [high - low for low, high in marks]


def from_messages(refs, parts):
    found = [refs[message][:, at : at + size] for message, at, _, size in parts]
    return found[0] if len(found) == 1 else jnp.concatenate(found, axis=1)


def to_messages(refs, parts, value):
    for message, at, begin, size in parts:
        refs[message][:, at : at + size] = value[:, begin : begin + size]


def forward(features, other_rows, up_weight, core, span, spans_of_tokens, numbers, after):
    low, high = span
    depth = up_weight.shape[0]
    tile = tile_of(_gcd(high - low, low), 1024)
    steps = (high - low) // tile
    count = other_rows.shape[0]
    first = spans_of_tokens[0][0]
    plans = [in_messages(steps, tile, number) for number in numbers]
    firsts = [0]
    for _, widths in plans:
        firsts.append(firsts[-1] + 1 + len(widths))

    def body(scalar_ref, inputs, outputs, scratch):
        rows = jnp.concatenate([inputs[0][...], inputs[1][...]], axis=0)
        product = jnp.dot(rows, inputs[2][...], preferred_element_type=F32)
        for n, (a, b) in enumerate(spans_of_tokens):
            outputs[firsts[n]][...] = product[a - first : b - first]
            send = product[count + a - first : count + b - first].astype(BF16)
            for step, parts in enumerate(plans[n][0]):

                @pl.when(pl.program_id(0) == step)
                def _(send=send, n=n, parts=parts):
                    to_messages(outputs[firsts[n] + 1 :], parts, send)

    out_specs, out_shape = [], []
    for (a, b), (_, widths) in zip(spans_of_tokens, plans):
        out_specs.append(pl.BlockSpec((b - a, tile), lambda i, *_: (0, i)))
        out_shape.append(jax.ShapeDtypeStruct((b - a, high - low), F32))
        out_specs += [pl.BlockSpec((b - a, width), lambda i, *_: (0, 0)) for width in widths]
        out_shape += [jax.ShapeDtypeStruct((b - a, width), BF16) for width in widths]
    *results, mark = ordered(
        "forward",
        body,
        after,
        [
            pl.BlockSpec(
                (pl.Element(count), pl.Element(depth)),
                lambda i, core_ref: (first, pl.multiple_of(core_ref[0] * depth, LANES)),
            ),
            pl.BlockSpec((count, depth), lambda i, *_: (0, 0)),
            pl.BlockSpec((depth, tile), lambda i, *_: (0, low // tile + i)),
        ],
        out_specs,
        out_shape,
        grid=(steps,),
        scalars=core,
    )(features, other_rows, up_weight)
    parts = [results[n:m] for n, m in zip(firsts[:-1], firsts[1:])]
    return [(part[0], part[1:]) for part in parts], mark


def _gcd(x, y):
    while y:
        x, y = y, x % y
    return x


def add_parts(own, messages, tile, after):
    count, total = own.shape
    where, _ = in_messages(total // tile, tile, len(messages))

    def body(scalar_ref, inputs, outputs, scratch):
        for step, parts in enumerate(where):

            @pl.when(pl.program_id(0) == step)
            def _(parts=parts):
                other = from_messages(inputs[1:], parts).astype(F32)
                outputs[0][...] = (inputs[0][...] + other).astype(BF16)

    tile_spec = pl.BlockSpec((count, tile), lambda i, *_: (0, i))
    return ordered(
        "add",
        body,
        after,
        [tile_spec] + [pl.BlockSpec(part.shape, lambda i, *_: (0, 0)) for part in messages],
        [tile_spec],
        [jax.ShapeDtypeStruct((count, total), BF16)],
        grid=(total // tile,),
    )(own, *messages)


def slope_rows(mine, theirs, out_grad, tokens, span, tile, after):
    (start_row, end_row), (low, high) = tokens, span
    count = end_row - start_row
    where, widths = in_messages((high - low) // tile, tile, SLOPE_MESSAGES)

    def body(scalar_ref, inputs, outputs, scratch):
        preact = inputs[0][...].astype(F32) + inputs[1][...].astype(F32)
        sigmoid_value = 0.5 * jnp.tanh(0.5 * preact) + 0.5
        rows = (
            inputs[2][...].astype(F32) * sigmoid_value * (1.0 + preact * (1.0 - sigmoid_value))
        ).astype(BF16)
        for step, parts in enumerate(where):

            @pl.when(pl.program_id(0) == step)
            def _(parts=parts):
                to_messages(outputs, parts, rows)

    tile_spec = pl.BlockSpec((count, tile), lambda i, *_: (0, i))
    *results, mark = ordered(
        "slope",
        body,
        after,
        [
            tile_spec,
            tile_spec,
            pl.BlockSpec(
                (pl.Element(count), pl.Element(tile)),
                lambda i, *_: (start_row, pl.multiple_of(low + i * tile, LANES)),
            ),
        ],
        [pl.BlockSpec((count, width), lambda i, *_: (0, 0)) for width in widths],
        [jax.ShapeDtypeStruct((count, width), BF16) for width in widths],
        grid=((high - low) // tile,),
    )(mine, theirs, out_grad)
    return results, mark


def backward(own_messages, other_messages, span, tile, up_weight, left_rows, total, place, blocks, last, after):
    low = span[0]
    depth = up_weight.shape[0]
    count = own_messages[0].shape[0]
    width = depth // blocks
    parts = 2 * blocks
    steps = (span[1] - low) // tile
    where, widths = in_messages(steps, tile, SLOPE_MESSAGES)
    messages = len(widths)

    def body(scalar_ref, inputs, outputs, scratch):
        step = pl.program_id(0)
        weight, left = inputs[:2]
        own_refs, other_refs = inputs[2 : 2 + messages], inputs[2 + messages : 2 + 2 * messages]
        sums, left_sums = scratch if last else outputs

        @pl.when(step == 0)
        def _():
            if total is None:
                sums[...] = jnp.zeros_like(sums)
                left_sums[...] = jnp.zeros_like(left_sums)
            else:
                sums[...] = inputs[-2][...]
                left_sums[...] = inputs[-1][...]

        for n, places in enumerate(where):

            @pl.when(step == n)
            def _(places=places):
                own = from_messages(own_refs, places)
                both = jnp.concatenate([own, from_messages(other_refs, places)], axis=0)
                for block in range(blocks):
                    product = contract_last(both, weight[block * width : (block + 1) * width, :])
                    sums[2 * block] += product[:count]
                    sums[2 * block + 1] += product[count:]
                left_sums[...] += contract_last(own, left[...])

        if last:

            @pl.when(step == steps - 1)
            def _():
                for n in range(blocks):
                    block = lax.rem(scalar_ref[0] + n, blocks)
                    for r in range(2):
                        held = scalar_ref[1] if r == 0 else 1 - scalar_ref[1]
                        at = pl.multiple_of(held * count, 16)
                        outputs[n][pl.ds(at, count), :] = sums[2 * block + r].astype(BF16)
                outputs[blocks][...] = left_sums[...]

    sums_shape, left_shape = (parts, count, width), (count, left_rows.shape[0])
    sums_spec = pl.BlockSpec(sums_shape, lambda i, *_: (0, 0, 0))
    left_spec = pl.BlockSpec(left_shape, lambda i, *_: (0, 0))
    in_specs = [
        pl.BlockSpec((depth, tile), lambda i, *_: (0, low // tile + i)),
        pl.BlockSpec((left_rows.shape[0], tile), lambda i, *_: (0, low // tile + i)),
    ]
    operands = [up_weight, left_rows, *own_messages, *other_messages]
    in_specs += [pl.BlockSpec((count, size), lambda i, *_: (0, 0)) for size in widths] * 2
    if total is not None:
        in_specs += [sums_spec, left_spec]
        operands += total
    if last:
        out_specs = [pl.BlockSpec((2 * count, width), lambda i, *_: (0, 0))] * blocks + [left_spec]
        out_shape = [jax.ShapeDtypeStruct((2 * count, width), BF16)] * blocks
        out_shape.append(jax.ShapeDtypeStruct(left_shape, F32))
        scratch = [pltpu.VMEM(sums_shape, F32), pltpu.VMEM(left_shape, F32)]
    else:
        out_specs = [sums_spec, left_spec]
        out_shape = [jax.ShapeDtypeStruct(sums_shape, F32), jax.ShapeDtypeStruct(left_shape, F32)]
        scratch = []
    *results, mark = ordered(
        "backward", body, after, in_specs, out_specs, out_shape, (steps,), scratch, place
    )(*operands)
    return results, mark


def exchange(message, n, blocks):
    pairs = []
    for t in range(lax.axis_size("tensor")):
        for c in range(2):
            pairs.append((2 * t + c, 2 * (blocks * c + (t + n) % blocks) + t // blocks))
    return lax.ppermute(message, ("tensor", "dp"), pairs)


def gathered_sum(arrived, core, after):
    count, width = arrived[0].shape[0] // 2, arrived[0].shape[1]

    def body(scalar_ref, inputs, outputs, scratch):
        for output, held in zip(outputs, (scalar_ref[0], 1 - scalar_ref[0])):
            rows = pl.ds(pl.multiple_of(held * count, 16), count)
            output[...] = sum(ref[rows, :].astype(F32) for ref in inputs).astype(output.dtype)

    spec = pl.BlockSpec((count, width), lambda i, *_: (0, 0))
    own, message, mark = ordered(
        "gathered_sum",
        body,
        after,
        [pl.BlockSpec(array.shape, lambda i, *_: (0, 0)) for array in arrived],
        [spec, spec],
        [jax.ShapeDtypeStruct((count, width), F32), jax.ShapeDtypeStruct((count, width), BF16)],
        scalars=core,
    )(*arrived)
    return own, lax.ppermute(message, "dp", [(0, 1), (1, 0)]), mark


def paired(features, up_weight, out_grad, left_factors, right_factors, token_ids, query_ids):
    query_count, rank_count = left_factors.shape[:2]
    left_rows = left_factors.reshape(query_count * rank_count, left_factors.shape[2])
    right_rows = right_factors.reshape(query_count * rank_count, right_factors.shape[2])
    token_count, hidden = out_grad.shape
    depth = up_weight.shape[0]
    blocks = lax.axis_size("tensor") // 2
    core = lax.axis_index("dp")
    swap = [(0, 1), (1, 0)]
    place = jnp.stack([lax.rem(lax.axis_index("tensor"), blocks), core]).astype(jnp.int32)

    tokens = cuts(token_count, 16, TOKEN_SHARES)
    groups = [(tokens[:1], cuts(hidden, LANES, HEAD_SHARES)), (tokens[1:], cuts(hidden, LANES, REST_SHARES))]

    core_ref = core.astype(jnp.int32).reshape(1)
    mark = jnp.zeros((8, LANES), F32)
    from_other, adds, mine, theirs, rows = {}, {}, {}, {}, {}
    totals, held, arrived, lefts, results = {}, {}, {}, {}, {}

    def run_half(g, mark):
        span = (groups[g][0][0][0], groups[g][0][-1][1])
        away, mark = half_of(features, span, depth, core_ref, [mark])
        from_other[g] = lax.ppermute(away, "dp", swap)
        return mark

    def run_forward(g, j, mark):
        token_spans, spans = groups[g]
        first = 0 if g == 0 else 1
        numbers = FORWARD_MESSAGES[first : first + len(token_spans)]
        results, mark = forward(
            features, from_other[g], up_weight, core_ref, spans[j], token_spans, numbers, [mark]
        )
        for t, (own, send) in enumerate(results):
            adds[first + t, j] = (own, [lax.ppermute(part, "dp", swap) for part in send])
        return mark

    def span_of(piece):
        return groups[min(piece[0], 1)][1][piece[1]]

    def tile_for(piece):
        low, high = span_of(piece)
        return tile_of(_gcd(high - low, low), 1024)

    def run_add(piece, mark, *after):
        own, messages = adds[piece]
        mine[piece], mark = add_parts(own, messages, tile_for(piece), [mark, *after])
        theirs[piece] = lax.ppermute(mine[piece], "query", swap)
        return mark

    def run_slope(piece, mark, *after):
        own, mark = slope_rows(
            mine[piece],
            theirs[piece],
            out_grad,
            tokens[piece[0]],
            span_of(piece),
            tile_for(piece),
            [mark, *after],
        )
        rows[piece] = (own, [lax.ppermute(part, "dp", swap) for part in own])
        return mark

    def run_backward(piece, last, mark, *after):
        t = piece[0]
        results, mark = backward(
            *rows[piece],
            span_of(piece),
            tile_for(piece),
            up_weight,
            left_rows,
            totals.get(t),
            place,
            blocks,
            last,
            [mark, *after],
        )
        if last:
            held[t], lefts[t] = results[:-1], results[-1]
        else:
            totals[t] = results
        return mark

    def send_sums(t):
        arrived[t] = [exchange(part, n, blocks) for n, part in enumerate(held[t])]

    def add_sums(t, mark):
        own, other, mark = gathered_sum(arrived[t], core_ref, [mark])
        results[t] = (own + other.astype(F32)).astype(BF16)
        return mark

    tensor_size = lax.axis_size("tensor")
    tensor_index = lax.axis_index("tensor")
    fold = tensor_size // 2
    owns = (tensor_index // fold == lax.axis_index("query")).astype(jnp.int32).reshape(1)
    where = jnp.stack([core, tensor_index % fold * right_rows.shape[1]]).astype(jnp.int32)
    back = [(b, a) for a, b in right_pairs(tensor_size)]

    def across(array, step):
        return lax.ppermute(array, "tensor", [(t, t ^ step) for t in range(tensor_size)])

    mark = run_half(0, mark)
    right_here = right_send(right_rows)
    mark = run_forward(0, 0, mark)
    mark = run_add((0, 0), mark, right_here)
    mark = run_forward(0, 1, mark)
    right_there = lax.ppermute(right_here, "dp", swap)
    mark = run_half(1, mark)
    right_own, for_other, mark = right_products(
        features, right_rows, right_here, right_there, where, [mark]
    )
    received = lax.ppermute(for_other, ("tensor", "query"), back)
    mark = run_add((0, 1), mark, theirs[0, 0], received)
    mark = run_slope((0, 0), mark)
    mark = run_forward(1, 0, mark)
    right_part, mark = right_choice(right_own, received, owns, [mark])
    right_other = across(right_part, 1)
    mark = run_add((1, 0), mark)
    mark = run_forward(1, 1, mark)
    mark = run_slope((0, 1), mark)
    mark = run_add((1, 1), mark)
    mark = run_backward((0, 0), False, mark)
    right_sum = right_part
    for step in range(1, tensor_size.bit_length() - 1):
        right_sum, message, mark = add_right(right_sum, right_other, [mark])
        right_other = across(message, 1 << step)
    mark = run_backward((0, 1), True, mark)
    send_sums(0)
    mark = run_slope((1, 0), mark, right_other)
    mark = run_backward((1, 0), False, mark)
    mark = run_add((2, 0), mark)
    mark = run_slope((1, 1), mark, arrived[0][0])
    mark = run_backward((1, 1), True, mark)
    send_sums(1)
    mark = run_add((2, 1), mark)
    mark = add_sums(0, mark)
    mark = run_slope((2, 0), mark)
    mark = run_backward((2, 0), False, mark)
    mark = run_slope((2, 1), mark, arrived[1][0])
    mark = run_backward((2, 1), True, mark)
    send_sums(2)
    mark = add_sums(1, mark)
    mark = add_sums(2, mark)

    right_sum = right_sum.astype(F32) + right_other.astype(F32)
    weighted, grads = 0.0, []
    for t, (low, high) in enumerate(tokens):
        membership = (
            token_ids[None, low:high] == jnp.arange(EXAMPLES, dtype=jnp.int32)[:, None]
        ).astype(F32)
        weighted = weighted + exact_dot(membership, lefts[t] * right_sum[low:high])
        grads.append(results[t])
    choice = column_choice(query_ids, query_count, rank_count)
    scores = lax.psum(exact_dot(weighted, choice) / rank_count, ("tensor", "dp"))
    return jnp.concatenate(grads, axis=0), scores


def broadcast(value, axis, source):
    kept = jnp.where(lax.axis_index(axis) == source, value, 0).astype(value.dtype)
    return lax.psum(kept, axis)


def general(features, up_weight, out_grad, left_factors, right_factors, token_ids, query_ids):
    query_count, rank_count = left_factors.shape[:2]
    local_rows = lax.all_gather(up_weight, "dp", axis=0, tiled=True)
    preact_part = jnp.dot(features, local_rows, preferred_element_type=jnp.float32)
    preact_share = lax.psum_scatter(preact_part, "query", scatter_dimension=0, tiled=True)
    share_rows = preact_share.shape[0]
    own_grad = lax.dynamic_slice_in_dim(
        out_grad, lax.axis_index("query") * share_rows, share_rows, 0
    )
    grad_rows = lax.all_gather(silu_slope(preact_share, own_grad), "query", axis=0, tiled=True)
    input_part = contract_last(grad_rows, local_rows)
    input_grad = lax.psum_scatter(input_part, "tensor", scatter_dimension=1, tiled=True).astype(
        jnp.bfloat16
    )
    fold_ratio = lax.axis_size("tensor") // lax.axis_size("query")
    tensor_index = lax.axis_index("tensor")
    block_width = right_factors.shape[2]
    feature_piece = lax.dynamic_slice_in_dim(
        features, tensor_index % fold_ratio * block_width, block_width, 1
    )
    feature_block = broadcast(feature_piece, "query", tensor_index // fold_ratio)
    left_proj = contract_last(
        grad_rows, left_factors.reshape(query_count * rank_count, left_factors.shape[2])
    )
    right_proj = contract_last(
        feature_block, right_factors.reshape(query_count * rank_count, block_width)
    )
    left_sum, right_sum = lax.psum((left_proj, right_proj), "tensor")
    membership = (token_ids[None, :] == jnp.arange(EXAMPLES, dtype=jnp.int32)[:, None]).astype(
        jnp.float32
    )
    weighted = exact_dot(membership, left_sum * right_sum)
    choice = column_choice(query_ids, query_count, rank_count)
    scores = lax.psum(exact_dot(weighted, choice) / rank_count, "dp")
    return (input_grad, scores)


def solution(mesh):
    size = mesh.shape
    is_paired = size["query"] == 2 and size["dp"] == 2 and size["tensor"] in (2, 4, 8, 16)
    return jax.shard_map(
        paired if is_paired else general,
        mesh=mesh,
        in_specs=(
            P(("groups", "dp"), "query"),
            P(("query", "dp"), "tensor"),
            P(("groups", "dp"), "tensor"),
            P("query", None, "tensor"),
            P("query", None, "tensor"),
            P(("groups", "dp")),
            P("query", None),
        ),
        out_specs=(P(("groups", "dp"), ("query", "tensor")), P("groups", "query")),
        check_vma=False,
    )
```

```python
import jax
import jax.numpy as jnp
from jax import lax
from jax.experimental import pallas as pl
from jax.experimental.pallas import tpu as pltpu
from jax.sharding import PartitionSpec as P

EXAMPLES = 16
LANES = 128
TOKEN_SHARES = (13, 12, 7)
HEAD_SHARES = (3, 4)
REST_SHARES = (4, 3)
FORWARD_MESSAGES = ((3, 2), (3, 2), (1, 1))
SLOPE_MESSAGES = ((2, 2), (3, 2), (2, 2))
VMEM_BYTES = 24 << 20
SMALL_VMEM_BYTES = 12 << 20
F32, BF16 = jnp.float32, jnp.bfloat16


def silu_slope(preact, grad_part):
    sigmoid_value = jax.nn.sigmoid(preact)
    return (
        grad_part.astype(jnp.float32) * sigmoid_value * (1.0 + preact * (1.0 - sigmoid_value))
    ).astype(jnp.bfloat16)


def contract_last(left_rows, right_rows):
    return lax.dot_general(
        left_rows, right_rows, (((1,), (1,)), ((), ())), preferred_element_type=jnp.float32
    )


def cuts(total, unit, shares):
    whole, marks, seen = sum(shares), [0], 0
    for share in shares:
        seen += share
        mark = total * seen // whole // unit * unit if seen < whole else total
        if mark > marks[-1]:
            marks.append(mark)
    return list(zip(marks[:-1], marks[1:]))


def column_choice(query_ids, query_count, rank_count):
    owner = jnp.arange(query_count * rank_count, dtype=jnp.int32) // rank_count
    return (owner[:, None] == query_ids[0][None, :]).astype(jnp.float32)


def exact_dot(a, b):
    return jnp.dot(a, b, precision=lax.Precision.HIGHEST, preferred_element_type=jnp.float32)


def right_pairs(tensor_size):
    fold = tensor_size // 2
    return [(2 * t + 1 - t // fold, 2 * t + t // fold) for t in range(tensor_size)]


def right_send(right_rows):
    half = right_rows.shape[0] // 2
    piece = lax.dynamic_slice_in_dim(right_rows, lax.axis_index("dp") * half, half, 0)
    return lax.ppermute(piece, ("tensor", "query"), right_pairs(lax.axis_size("tensor")))


def right_products(features, right_rows, here, there, where, after):
    rows, depth = right_rows.shape
    half = rows // 2
    count = features.shape[0]

    def body(scalar_ref, inputs, outputs, scratch):
        block = inputs[0][...]
        outputs[0][...] = contract_last(block, inputs[1][...])
        first, second = contract_last(block, inputs[2][...]), contract_last(block, inputs[3][...])
        is_first = scalar_ref[0] == 0
        outputs[1][:, :half] = jnp.where(is_first, first, second).astype(BF16)
        outputs[1][:, half:] = jnp.where(is_first, second, first).astype(BF16)

    whole = pl.BlockSpec((count, rows), lambda i, *_: (0, 0))
    own, for_other, mark = ordered(
        "right",
        body,
        after,
        [
            pl.BlockSpec(
                (pl.Element(count), pl.Element(depth)),
                lambda i, where_ref: (0, pl.multiple_of(where_ref[1], LANES)),
            ),
            pl.BlockSpec((rows, depth), lambda i, *_: (0, 0)),
            pl.BlockSpec((half, depth), lambda i, *_: (0, 0)),
            pl.BlockSpec((half, depth), lambda i, *_: (0, 0)),
        ],
        [whole, whole],
        [jax.ShapeDtypeStruct((count, rows), F32), jax.ShapeDtypeStruct((count, rows), BF16)],
        scalars=where,
    )(features, right_rows, here, there)
    return own, for_other, mark


def right_choice(own, received, owns, after):
    def body(scalar_ref, inputs, outputs, scratch):
        outputs[0][...] = jnp.where(
            scalar_ref[0] == 1, inputs[0][...], inputs[1][...].astype(F32)
        ).astype(BF16)

    whole = pl.BlockSpec(own.shape, lambda i, *_: (0, 0))
    return ordered(
        "right_choice",
        body,
        after,
        [whole, whole],
        [whole],
        [jax.ShapeDtypeStruct(own.shape, BF16)],
        scalars=owns,
        vmem=SMALL_VMEM_BYTES,
    )(own, received)


def tile_of(width, limit):
    return max(t for t in range(LANES, limit + 1, LANES) if width % t == 0)


def fixed(shape):
    return pl.BlockSpec(shape, lambda i, *_: (0,) * len(shape), pipeline_mode=pl.Buffered(1))


def ordered(name, body, after, in_specs, out_specs, out_shape, grid=(1,), scratch_shapes=(), scalars=None, vmem=VMEM_BYTES):
    def kernel(scalar_ref, *refs):
        refs = refs[len(after) :]
        inputs, rest = refs[: len(in_specs)], refs[len(in_specs) :]
        outputs, own_mark, scratch = (
            rest[: len(out_specs)],
            rest[len(out_specs)],
            rest[len(out_specs) + 1 :],
        )
        own_mark[...] = jnp.zeros_like(own_mark)
        body(scalar_ref, inputs, outputs, scratch)

    mark_spec = pl.BlockSpec((8, LANES), lambda *ids: (0, 0))

    if scalars is None:
        scalars = jnp.zeros((1,), jnp.int32)

    def call(*operands):
        return pl.pallas_call(
            kernel,
            grid_spec=pltpu.PrefetchScalarGridSpec(
                num_scalar_prefetch=1,
                grid=grid,
                in_specs=[pl.BlockSpec(memory_space=pl.ANY)] * len(after) + list(in_specs),
                out_specs=list(out_specs) + [mark_spec],
                scratch_shapes=list(scratch_shapes),
            ),
            out_shape=list(out_shape) + [jax.ShapeDtypeStruct((8, LANES), F32)],
            compiler_params=pltpu.CompilerParams(vmem_limit_bytes=vmem),
            cost_estimate=pl.CostEstimate(flops=1, bytes_accessed=1, transcendentals=0),
            name=name,
        )(scalars, *after, *operands)

    return call


def half_of(features, tokens, depth, core, after):
    low, high = tokens

    def body(scalar_ref, inputs, outputs, scratch):
        outputs[0][...] = inputs[0][...]

    return ordered(
        "half",
        body,
        after,
        [
            pl.BlockSpec(
                (pl.Element(high - low), pl.Element(depth)),
                lambda i, core_ref: (low, pl.multiple_of((1 - core_ref[0]) * depth, LANES)),
            )
        ],
        [pl.BlockSpec((high - low, depth), lambda i, *_: (0, 0))],
        [jax.ShapeDtypeStruct((high - low, depth), features.dtype)],
        scalars=core,
        vmem=SMALL_VMEM_BYTES,
    )(features)


def add_right(own, received, after):
    def body(scalar_ref, inputs, outputs, scratch):
        total = inputs[0][...].astype(F32) + inputs[1][...].astype(F32)
        outputs[0][...] = total
        outputs[1][...] = total.astype(BF16)

    whole = pl.BlockSpec(own.shape, lambda i, *_: (0, 0))
    total, message, mark = ordered(
        "add_right",
        body,
        after,
        [whole, whole],
        [whole, whole],
        [jax.ShapeDtypeStruct(own.shape, F32), jax.ShapeDtypeStruct(own.shape, BF16)],
        vmem=SMALL_VMEM_BYTES,
    )(own, received)
    return total, message, mark


def in_messages(steps, tile, number):
    marks = cuts(steps * tile, LANES, (1,) * number)
    where = []
    for step in range(steps):
        parts = []
        for message, (low, high) in enumerate(marks):
            begin, end = max(low, step * tile), min(high, (step + 1) * tile)
            if begin < end:
                parts.append((message, begin - low, begin - step * tile, end - begin))
        where.append(parts)
    return where, [high - low for low, high in marks]


def from_messages(refs, parts):
    found = [refs[message][:, at : at + size] for message, at, _, size in parts]
    return found[0] if len(found) == 1 else jnp.concatenate(found, axis=1)


def to_messages(refs, parts, value):
    for message, at, begin, size in parts:
        refs[message][:, at : at + size] = value[:, begin : begin + size]


def forward(features, other_rows, up_weight, core, span, spans_of_tokens, numbers, after):
    low, high = span
    depth = up_weight.shape[0]
    tile = tile_of(_gcd(high - low, low), 1024)
    steps = (high - low) // tile
    count = other_rows.shape[0]
    first = spans_of_tokens[0][0]
    plans = [in_messages(steps, tile, number) for number in numbers]
    firsts = [0]
    for _, widths in plans:
        firsts.append(firsts[-1] + 1 + len(widths))

    def body(scalar_ref, inputs, outputs, scratch):
        rows = jnp.concatenate([inputs[0][...], inputs[1][...]], axis=0)
        product = jnp.dot(rows, inputs[2][...], preferred_element_type=F32)
        for n, (a, b) in enumerate(spans_of_tokens):
            outputs[firsts[n]][...] = product[a - first : b - first].astype(BF16)
            send = product[count + a - first : count + b - first].astype(BF16)
            for step, parts in enumerate(plans[n][0]):

                @pl.when(pl.program_id(0) == step)
                def _(send=send, n=n, parts=parts):
                    to_messages(outputs[firsts[n] + 1 :], parts, send)

    out_specs, out_shape = [], []
    for (a, b), (_, widths) in zip(spans_of_tokens, plans):
        out_specs.append(pl.BlockSpec((b - a, tile), lambda i, *_: (0, i)))
        out_shape.append(jax.ShapeDtypeStruct((b - a, high - low), BF16))
        out_specs += [pl.BlockSpec((b - a, width), lambda i, *_: (0, 0)) for width in widths]
        out_shape += [jax.ShapeDtypeStruct((b - a, width), BF16) for width in widths]
    *results, mark = ordered(
        "forward",
        body,
        after,
        [
            fixed((count, depth))
            if features.shape == (count, depth)
            else pl.BlockSpec(
                (pl.Element(count), pl.Element(depth)),
                lambda i, core_ref: (first, pl.multiple_of(core_ref[0] * depth, LANES)),
                pipeline_mode=pl.Buffered(1),
            ),
            fixed((count, depth)),
            pl.BlockSpec((depth, tile), lambda i, *_: (0, low // tile + i)),
        ],
        out_specs,
        out_shape,
        grid=(steps,),
        scalars=core,
    )(features, other_rows, up_weight)
    parts = [results[n:m] for n, m in zip(firsts[:-1], firsts[1:])]
    return [(part[0], part[1:]) for part in parts], mark


def _gcd(x, y):
    while y:
        x, y = y, x % y
    return x


def add_parts(own, messages, tile, after):
    count, total = own.shape
    where, _ = in_messages(total // tile, tile, len(messages))

    def body(scalar_ref, inputs, outputs, scratch):
        for step, parts in enumerate(where):

            @pl.when(pl.program_id(0) == step)
            def _(parts=parts):
                other = from_messages(inputs[1:], parts).astype(F32)
                outputs[0][...] = (inputs[0][...].astype(F32) + other).astype(BF16)

    tile_spec = pl.BlockSpec((count, tile), lambda i, *_: (0, i))
    return ordered(
        "add",
        body,
        after,
        [tile_spec] + [fixed(part.shape) for part in messages],
        [tile_spec],
        [jax.ShapeDtypeStruct((count, total), BF16)],
        grid=(total // tile,),
        vmem=SMALL_VMEM_BYTES,
    )(own, *messages)


def slope_rows(mine, theirs, out_grad, tokens, span, tile, number, after):
    (start_row, end_row), (low, high) = tokens, span
    count = end_row - start_row
    where, widths = in_messages((high - low) // tile, tile, number)

    def body(scalar_ref, inputs, outputs, scratch):
        preact = inputs[0][...].astype(F32) + inputs[1][...].astype(F32)
        sigmoid_value = 0.5 * jnp.tanh(0.5 * preact) + 0.5
        rows = (
            inputs[2][...].astype(F32) * sigmoid_value * (1.0 + preact * (1.0 - sigmoid_value))
        ).astype(BF16)
        for step, parts in enumerate(where):

            @pl.when(pl.program_id(0) == step)
            def _(parts=parts):
                to_messages(outputs, parts, rows)

    tile_spec = pl.BlockSpec((count, tile), lambda i, *_: (0, i))
    *results, mark = ordered(
        "slope",
        body,
        after,
        [
            tile_spec,
            tile_spec,
            pl.BlockSpec(
                (pl.Element(count), pl.Element(tile)),
                lambda i, *_: (start_row, pl.multiple_of(low + i * tile, LANES)),
            ),
        ],
        [pl.BlockSpec((count, width), lambda i, *_: (0, 0)) for width in widths],
        [jax.ShapeDtypeStruct((count, width), BF16) for width in widths],
        grid=((high - low) // tile,),
        vmem=SMALL_VMEM_BYTES,
    )(mine, theirs, out_grad)
    return results, mark


def backward(own_messages, other_messages, span, tile, up_weight, left_rows, total, place, blocks, last, after):
    low = span[0]
    depth = up_weight.shape[0]
    count = own_messages[0].shape[0]
    width = depth // blocks
    parts = 2 * blocks
    steps = (span[1] - low) // tile
    where, widths = in_messages(steps, tile, len(own_messages))
    messages = len(widths)

    def body(scalar_ref, inputs, outputs, scratch):
        step = pl.program_id(0)
        weight, left = inputs[:2]
        own_refs, other_refs = inputs[2 : 2 + messages], inputs[2 + messages : 2 + 2 * messages]
        sums, left_sums = scratch if last else outputs

        @pl.when(step == 0)
        def _():
            if total is None:
                sums[...] = jnp.zeros_like(sums)
                left_sums[...] = jnp.zeros_like(left_sums)
            else:
                sums[...] = inputs[-2][...]
                left_sums[...] = inputs[-1][...]

        for n, places in enumerate(where):

            @pl.when(step == n)
            def _(places=places):
                own = from_messages(own_refs, places)
                both = jnp.concatenate([own, from_messages(other_refs, places)], axis=0)
                for block in range(blocks):
                    product = contract_last(both, weight[block * width : (block + 1) * width, :])
                    sums[2 * block] += product[:count]
                    sums[2 * block + 1] += product[count:]
                left_sums[...] += contract_last(own, left[...])

        if last:

            @pl.when(step == steps - 1)
            def _():
                for n in range(blocks):
                    block = lax.rem(scalar_ref[0] + n, blocks)
                    for r in range(2):
                        held = scalar_ref[1] if r == 0 else 1 - scalar_ref[1]
                        at = pl.multiple_of(held * count, 16)
                        outputs[n][pl.ds(at, count), :] = sums[2 * block + r].astype(BF16)
                outputs[blocks][...] = left_sums[...]

    sums_shape, left_shape = (parts, count, width), (count, left_rows.shape[0])
    sums_spec = pl.BlockSpec(sums_shape, lambda i, *_: (0, 0, 0))
    left_spec = pl.BlockSpec(left_shape, lambda i, *_: (0, 0))
    in_specs = [
        pl.BlockSpec((depth, tile), lambda i, *_: (0, low // tile + i)),
        pl.BlockSpec((left_rows.shape[0], tile), lambda i, *_: (0, low // tile + i)),
    ]
    operands = [up_weight, left_rows, *own_messages, *other_messages]
    in_specs += [fixed((count, size)) for size in widths] * 2
    if total is not None:
        in_specs += [fixed(sums_shape), fixed(left_shape)]
        operands += total
    if last:
        out_specs = [pl.BlockSpec((2 * count, width), lambda i, *_: (0, 0))] * blocks + [left_spec]
        out_shape = [jax.ShapeDtypeStruct((2 * count, width), BF16)] * blocks
        out_shape.append(jax.ShapeDtypeStruct(left_shape, F32))
        scratch = [pltpu.VMEM(sums_shape, F32), pltpu.VMEM(left_shape, F32)]
    else:
        out_specs = [sums_spec, left_spec]
        out_shape = [jax.ShapeDtypeStruct(sums_shape, F32), jax.ShapeDtypeStruct(left_shape, F32)]
        scratch = []
    *results, mark = ordered(
        "backward", body, after, in_specs, out_specs, out_shape, (steps,), scratch, place
    )(*operands)
    return results, mark


def exchange(message, n, blocks):
    pairs = []
    for t in range(lax.axis_size("tensor")):
        for c in range(2):
            pairs.append((2 * t + c, 2 * (blocks * c + (t + n) % blocks) + t // blocks))
    return lax.ppermute(message, ("tensor", "dp"), pairs)


def gathered_sum(arrived, core, after):
    count, width = arrived[0].shape[0] // 2, arrived[0].shape[1]

    def body(scalar_ref, inputs, outputs, scratch):
        for output, held in zip(outputs, (scalar_ref[0], 1 - scalar_ref[0])):
            rows = pl.ds(pl.multiple_of(held * count, 16), count)
            output[...] = sum(ref[rows, :].astype(F32) for ref in inputs).astype(output.dtype)

    spec = pl.BlockSpec((count, width), lambda i, *_: (0, 0))
    own, message, mark = ordered(
        "gathered_sum",
        body,
        after,
        [pl.BlockSpec(array.shape, lambda i, *_: (0, 0)) for array in arrived],
        [spec, spec],
        [jax.ShapeDtypeStruct((count, width), F32), jax.ShapeDtypeStruct((count, width), BF16)],
        scalars=core,
    )(*arrived)
    return own, lax.ppermute(message, "dp", [(0, 1), (1, 0)]), mark


def paired(features, up_weight, out_grad, left_factors, right_factors, token_ids, query_ids):
    query_count, rank_count = left_factors.shape[:2]
    left_rows = left_factors.reshape(query_count * rank_count, left_factors.shape[2])
    right_rows = right_factors.reshape(query_count * rank_count, right_factors.shape[2])
    token_count, hidden = out_grad.shape
    depth = up_weight.shape[0]
    blocks = lax.axis_size("tensor") // 2
    core = lax.axis_index("dp")
    swap = [(0, 1), (1, 0)]
    place = jnp.stack([lax.rem(lax.axis_index("tensor"), blocks), core]).astype(jnp.int32)

    tokens = cuts(token_count, 16, TOKEN_SHARES)
    groups = [(tokens[:1], cuts(hidden, LANES, HEAD_SHARES)), (tokens[1:], cuts(hidden, LANES, REST_SHARES))]

    core_ref = core.astype(jnp.int32).reshape(1)
    mark = jnp.zeros((8, LANES), F32)
    from_other, adds, mine, theirs, rows = {}, {}, {}, {}, {}
    totals, held, arrived, lefts, results = {}, {}, {}, {}, {}

    def run_half(g, mark):
        span = (groups[g][0][0][0], groups[g][0][-1][1])
        away, mark = half_of(features, span, depth, core_ref, [mark])
        from_other[g] = lax.ppermute(away, "dp", swap)
        return mark

    low, high = tokens[0]
    first_own = lax.dynamic_slice(features, (low, core * depth), (high - low, depth))
    first_away = lax.dynamic_slice(features, (low, (1 - core) * depth), (high - low, depth))

    def run_forward(g, j, mark):
        token_spans, spans = groups[g]
        first = 0 if g == 0 else 1
        numbers = [FORWARD_MESSAGES[first + t][j] for t in range(len(token_spans))]
        results, mark = forward(
            features if g else first_own, from_other[g], up_weight, core_ref, spans[j], token_spans, numbers, [mark]
        )
        for t, (own, send) in enumerate(results):
            adds[first + t, j] = (own, [lax.ppermute(part, "dp", swap) for part in send])
        return mark

    def span_of(piece):
        return groups[min(piece[0], 1)][1][piece[1]]

    def tile_for(piece):
        low, high = span_of(piece)
        return tile_of(_gcd(high - low, low), 1024)

    def run_add(piece, mark, *after):
        own, messages = adds[piece]
        mine[piece], mark = add_parts(own, messages, tile_for(piece), [mark, *after])
        theirs[piece] = lax.ppermute(mine[piece], "query", swap)
        return mark

    def run_slope(piece, mark, *after):
        own, mark = slope_rows(
            mine[piece],
            theirs[piece],
            out_grad,
            tokens[piece[0]],
            span_of(piece),
            tile_for(piece),
            SLOPE_MESSAGES[piece[0]][piece[1]],
            [mark, *after],
        )
        rows[piece] = (own, [lax.ppermute(part, "dp", swap) for part in own])
        return mark

    def run_backward(piece, last, mark, *after):
        t = piece[0]
        results, mark = backward(
            *rows[piece],
            span_of(piece),
            tile_for(piece),
            up_weight,
            left_rows,
            totals.get(t),
            place,
            blocks,
            last,
            [mark, *after],
        )
        if last:
            held[t], lefts[t] = results[:-1], results[-1]
        else:
            totals[t] = results
        return mark

    def send_sums(t):
        arrived[t] = [exchange(part, n, blocks) for n, part in enumerate(held[t])]

    def add_sums(t, mark):
        own, other, mark = gathered_sum(arrived[t], core_ref, [mark])
        results[t] = (own + other.astype(F32)).astype(BF16)
        return mark

    tensor_size = lax.axis_size("tensor")
    tensor_index = lax.axis_index("tensor")
    fold = tensor_size // 2
    owns = (tensor_index // fold == lax.axis_index("query")).astype(jnp.int32).reshape(1)
    where = jnp.stack([core, tensor_index % fold * right_rows.shape[1]]).astype(jnp.int32)
    back = [(b, a) for a, b in right_pairs(tensor_size)]

    def across(array, step):
        return lax.ppermute(array, "tensor", [(t, t ^ step) for t in range(tensor_size)])

    from_other[0] = lax.ppermute(first_away, "dp", swap)
    right_here = right_send(right_rows)
    mark = run_forward(0, 0, mark)
    mark = run_add((0, 0), mark, right_here)
    mark = run_forward(0, 1, mark)
    right_there = lax.ppermute(right_here, "dp", swap)
    mark = run_half(1, mark)
    right_own, for_other, mark = right_products(
        features, right_rows, right_here, right_there, where, [mark]
    )
    received = lax.ppermute(for_other, ("tensor", "query"), back)
    mark = run_add((0, 1), mark, theirs[0, 0], received)
    mark = run_slope((0, 0), mark)
    mark = run_forward(1, 0, mark)
    right_part, mark = right_choice(right_own, received, owns, [mark])
    right_other = across(right_part, 1)
    mark = run_add((1, 0), mark)
    mark = run_forward(1, 1, mark)
    mark = run_slope((0, 1), mark)
    mark = run_add((1, 1), mark)
    mark = run_backward((0, 0), False, mark)
    right_sum = right_part
    for step in range(1, tensor_size.bit_length() - 1):
        right_sum, message, mark = add_right(right_sum, right_other, [mark])
        right_other = across(message, 1 << step)
    mark = run_backward((0, 1), True, mark, *adds[2, 0][1])
    send_sums(0)
    mark = run_slope((1, 0), mark, right_other)
    mark = run_backward((1, 0), False, mark)
    mark = run_add((2, 0), mark)
    mark = run_slope((1, 1), mark, arrived[0][0])
    mark = run_backward((1, 1), True, mark)
    send_sums(1)
    mark = run_add((2, 1), mark)
    mark = add_sums(0, mark)
    mark = run_slope((2, 0), mark)
    mark = run_backward((2, 0), False, mark)
    mark = run_slope((2, 1), mark, arrived[1][0])
    mark = run_backward((2, 1), True, mark)
    send_sums(2)
    mark = add_sums(1, mark)
    mark = add_sums(2, mark)

    right_sum = right_sum.astype(F32) + right_other.astype(F32)
    weighted, grads = 0.0, []
    for t, (low, high) in enumerate(tokens):
        membership = (
            token_ids[None, low:high] == jnp.arange(EXAMPLES, dtype=jnp.int32)[:, None]
        ).astype(F32)
        weighted = weighted + exact_dot(membership, lefts[t] * right_sum[low:high])
        grads.append(results[t])
    choice = column_choice(query_ids, query_count, rank_count)
    scores = lax.psum(exact_dot(weighted, choice) / rank_count, ("tensor", "dp"))
    return jnp.concatenate(grads, axis=0), scores


def broadcast(value, axis, source):
    kept = jnp.where(lax.axis_index(axis) == source, value, 0).astype(value.dtype)
    return lax.psum(kept, axis)


def general(features, up_weight, out_grad, left_factors, right_factors, token_ids, query_ids):
    query_count, rank_count = left_factors.shape[:2]
    local_rows = lax.all_gather(up_weight, "dp", axis=0, tiled=True)
    preact_part = jnp.dot(features, local_rows, preferred_element_type=jnp.float32)
    preact_share = lax.psum_scatter(preact_part, "query", scatter_dimension=0, tiled=True)
    share_rows = preact_share.shape[0]
    own_grad = lax.dynamic_slice_in_dim(
        out_grad, lax.axis_index("query") * share_rows, share_rows, 0
    )
    grad_rows = lax.all_gather(silu_slope(preact_share, own_grad), "query", axis=0, tiled=True)
    input_part = contract_last(grad_rows, local_rows)
    input_grad = lax.psum_scatter(input_part, "tensor", scatter_dimension=1, tiled=True).astype(
        jnp.bfloat16
    )
    fold_ratio = lax.axis_size("tensor") // lax.axis_size("query")
    tensor_index = lax.axis_index("tensor")
    block_width = right_factors.shape[2]
    feature_piece = lax.dynamic_slice_in_dim(
        features, tensor_index % fold_ratio * block_width, block_width, 1
    )
    feature_block = broadcast(feature_piece, "query", tensor_index // fold_ratio)
    left_proj = contract_last(
        grad_rows, left_factors.reshape(query_count * rank_count, left_factors.shape[2])
    )
    right_proj = contract_last(
        feature_block, right_factors.reshape(query_count * rank_count, block_width)
    )
    left_sum, right_sum = lax.psum((left_proj, right_proj), "tensor")
    membership = (token_ids[None, :] == jnp.arange(EXAMPLES, dtype=jnp.int32)[:, None]).astype(
        jnp.float32
    )
    weighted = exact_dot(membership, left_sum * right_sum)
    choice = column_choice(query_ids, query_count, rank_count)
    scores = lax.psum(exact_dot(weighted, choice) / rank_count, "dp")
    return (input_grad, scores)


def solution(mesh):
    size = mesh.shape
    is_paired = size["query"] == 2 and size["dp"] == 2 and size["tensor"] in (2, 4, 8, 16)
    return jax.shard_map(
        paired if is_paired else general,
        mesh=mesh,
        in_specs=(
            P(("groups", "dp"), "query"),
            P(("query", "dp"), "tensor"),
            P(("groups", "dp"), "tensor"),
            P("query", None, "tensor"),
            P("query", None, "tensor"),
            P(("groups", "dp")),
            P("query", None),
        ),
        out_specs=(P(("groups", "dp"), ("query", "tensor")), P("groups", "query")),
        check_vma=False,
    )
```

```python
import jax
import jax.numpy as jnp
from jax import lax
from jax.experimental import pallas as pl
from jax.experimental.pallas import tpu as pltpu
from jax.sharding import PartitionSpec as P

EXAMPLES = 16
LANES = 128
TOKEN_SHARES = (13, 12, 7)
HEAD_SHARES = (3, 4)
REST_SHARES = (4, 3)
FORWARD_MESSAGES = ((3, 2), (3, 2), (1, 1))
SLOPE_MESSAGES = ((2, 2), (3, 2), (2, 2))
VMEM_BYTES = 24 << 20
SMALL_VMEM_BYTES = 12 << 20
F32, BF16 = jnp.float32, jnp.bfloat16


def silu_slope(preact, grad_part):
    sigmoid_value = jax.nn.sigmoid(preact)
    return (
        grad_part.astype(jnp.float32) * sigmoid_value * (1.0 + preact * (1.0 - sigmoid_value))
    ).astype(jnp.bfloat16)


def contract_last(left_rows, right_rows):
    return lax.dot_general(
        left_rows, right_rows, (((1,), (1,)), ((), ())), preferred_element_type=jnp.float32
    )


def cuts(total, unit, shares):
    whole, marks, seen = sum(shares), [0], 0
    for share in shares:
        seen += share
        mark = total * seen // whole // unit * unit if seen < whole else total
        if mark > marks[-1]:
            marks.append(mark)
    return list(zip(marks[:-1], marks[1:]))


def column_choice(query_ids, query_count, rank_count):
    owner = jnp.arange(query_count * rank_count, dtype=jnp.int32) // rank_count
    return (owner[:, None] == query_ids[0][None, :]).astype(jnp.float32)


def exact_dot(a, b):
    return jnp.dot(a, b, precision=lax.Precision.HIGHEST, preferred_element_type=jnp.float32)


def right_pairs(tensor_size):
    fold = tensor_size // 2
    return [(2 * t + 1 - t // fold, 2 * t + t // fold) for t in range(tensor_size)]


def right_send(right_rows):
    half = right_rows.shape[0] // 2
    piece = lax.dynamic_slice_in_dim(right_rows, lax.axis_index("dp") * half, half, 0)
    return lax.ppermute(piece, ("tensor", "query"), right_pairs(lax.axis_size("tensor")))


def right_products(features, right_rows, here, there, where, after):
    rows, depth = right_rows.shape
    half = rows // 2
    count = features.shape[0]

    def body(scalar_ref, inputs, outputs, scratch):
        block = inputs[0][...]
        outputs[0][...] = contract_last(block, inputs[1][...])
        first, second = contract_last(block, inputs[2][...]), contract_last(block, inputs[3][...])
        is_first = scalar_ref[0] == 0
        outputs[1][:, :half] = jnp.where(is_first, first, second).astype(BF16)
        outputs[1][:, half:] = jnp.where(is_first, second, first).astype(BF16)

    whole = pl.BlockSpec((count, rows), lambda i, *_: (0, 0))
    own, for_other, mark = ordered(
        "right",
        body,
        after,
        [
            pl.BlockSpec(
                (pl.Element(count), pl.Element(depth)),
                lambda i, where_ref: (0, pl.multiple_of(where_ref[1], LANES)),
            ),
            pl.BlockSpec((rows, depth), lambda i, *_: (0, 0)),
            pl.BlockSpec((half, depth), lambda i, *_: (0, 0)),
            pl.BlockSpec((half, depth), lambda i, *_: (0, 0)),
        ],
        [whole, whole],
        [jax.ShapeDtypeStruct((count, rows), F32), jax.ShapeDtypeStruct((count, rows), BF16)],
        scalars=where,
    )(features, right_rows, here, there)
    return own, for_other, mark


def right_choice(own, received, owns, after):
    def body(scalar_ref, inputs, outputs, scratch):
        outputs[0][...] = jnp.where(
            scalar_ref[0] == 1, inputs[0][...], inputs[1][...].astype(F32)
        ).astype(BF16)

    whole = pl.BlockSpec(own.shape, lambda i, *_: (0, 0))
    return ordered(
        "right_choice",
        body,
        after,
        [whole, whole],
        [whole],
        [jax.ShapeDtypeStruct(own.shape, BF16)],
        scalars=owns,
        vmem=SMALL_VMEM_BYTES,
    )(own, received)


def tile_of(width, limit):
    return max(t for t in range(LANES, limit + 1, LANES) if width % t == 0)


def fixed(shape):
    return pl.BlockSpec(shape, lambda i, *_: (0,) * len(shape), pipeline_mode=pl.Buffered(1))


def ordered(name, body, after, in_specs, out_specs, out_shape, grid=(1,), scratch_shapes=(), scalars=None, vmem=VMEM_BYTES, aliases=()):
    def kernel(scalar_ref, *refs):
        refs = refs[len(after) :]
        inputs, rest = refs[: len(in_specs)], refs[len(in_specs) :]
        outputs, own_mark, scratch = (
            rest[: len(out_specs)],
            rest[len(out_specs)],
            rest[len(out_specs) + 1 :],
        )
        own_mark[...] = jnp.zeros_like(own_mark)
        body(scalar_ref, inputs, outputs, scratch)

    mark_spec = pl.BlockSpec((8, LANES), lambda *ids: (0, 0))

    if scalars is None:
        scalars = jnp.zeros((1,), jnp.int32)

    def call(*operands):
        return pl.pallas_call(
            kernel,
            grid_spec=pltpu.PrefetchScalarGridSpec(
                num_scalar_prefetch=1,
                grid=grid,
                in_specs=[pl.BlockSpec(memory_space=pl.ANY)] * len(after) + list(in_specs),
                out_specs=list(out_specs) + [mark_spec],
                scratch_shapes=list(scratch_shapes),
            ),
            out_shape=list(out_shape) + [jax.ShapeDtypeStruct((8, LANES), F32)],
            compiler_params=pltpu.CompilerParams(vmem_limit_bytes=vmem),
            cost_estimate=pl.CostEstimate(flops=1, bytes_accessed=1, transcendentals=0),
            name=name,
            input_output_aliases={1 + len(after) + source: target for source, target in aliases},
        )(scalars, *after, *operands)

    return call


def half_of(features, tokens, depth, core, after):
    low, high = tokens

    def body(scalar_ref, inputs, outputs, scratch):
        outputs[0][...] = inputs[0][...]

    return ordered(
        "half",
        body,
        after,
        [
            pl.BlockSpec(
                (pl.Element(high - low), pl.Element(depth)),
                lambda i, core_ref: (low, pl.multiple_of((1 - core_ref[0]) * depth, LANES)),
            )
        ],
        [pl.BlockSpec((high - low, depth), lambda i, *_: (0, 0))],
        [jax.ShapeDtypeStruct((high - low, depth), features.dtype)],
        scalars=core,
        vmem=SMALL_VMEM_BYTES,
    )(features)


def add_right(own, received, after):
    def body(scalar_ref, inputs, outputs, scratch):
        total = inputs[0][...].astype(F32) + inputs[1][...].astype(F32)
        outputs[0][...] = total
        outputs[1][...] = total.astype(BF16)

    whole = pl.BlockSpec(own.shape, lambda i, *_: (0, 0))
    total, message, mark = ordered(
        "add_right",
        body,
        after,
        [whole, whole],
        [whole, whole],
        [jax.ShapeDtypeStruct(own.shape, F32), jax.ShapeDtypeStruct(own.shape, BF16)],
        vmem=SMALL_VMEM_BYTES,
    )(own, received)
    return total, message, mark


def in_messages(steps, tile, number):
    marks = cuts(steps * tile, LANES, (1,) * number)
    where = []
    for step in range(steps):
        parts = []
        for message, (low, high) in enumerate(marks):
            begin, end = max(low, step * tile), min(high, (step + 1) * tile)
            if begin < end:
                parts.append((message, begin - low, begin - step * tile, end - begin))
        where.append(parts)
    return where, [high - low for low, high in marks]


def from_messages(refs, parts):
    found = [refs[message][:, at : at + size] for message, at, _, size in parts]
    return found[0] if len(found) == 1 else jnp.concatenate(found, axis=1)


def to_messages(refs, parts, value):
    for message, at, begin, size in parts:
        refs[message][:, at : at + size] = value[:, begin : begin + size]


def forward(features, other_rows, up_weight, core, span, spans_of_tokens, numbers, after):
    low, high = span
    depth = up_weight.shape[0]
    tile = tile_of(_gcd(high - low, low), 1024)
    steps = (high - low) // tile
    count = other_rows.shape[0]
    first = spans_of_tokens[0][0]
    plans = [in_messages(steps, tile, number) for number in numbers]
    firsts = [0]
    for _, widths in plans:
        firsts.append(firsts[-1] + 1 + len(widths))

    def body(scalar_ref, inputs, outputs, scratch):
        rows = jnp.concatenate([inputs[0][...], inputs[1][...]], axis=0)
        product = jnp.dot(rows, inputs[2][...], preferred_element_type=F32)
        for n, (a, b) in enumerate(spans_of_tokens):
            outputs[firsts[n]][...] = product[a - first : b - first].astype(BF16)
            send = product[count + a - first : count + b - first].astype(BF16)
            for step, parts in enumerate(plans[n][0]):

                @pl.when(pl.program_id(0) == step)
                def _(send=send, n=n, parts=parts):
                    to_messages(outputs[firsts[n] + 1 :], parts, send)

    out_specs, out_shape = [], []
    for (a, b), (_, widths) in zip(spans_of_tokens, plans):
        out_specs.append(pl.BlockSpec((b - a, tile), lambda i, *_: (0, i)))
        out_shape.append(jax.ShapeDtypeStruct((b - a, high - low), BF16))
        out_specs += [pl.BlockSpec((b - a, width), lambda i, *_: (0, 0)) for width in widths]
        out_shape += [jax.ShapeDtypeStruct((b - a, width), BF16) for width in widths]
    *results, mark = ordered(
        "forward",
        body,
        after,
        [
            fixed((count, depth))
            if features.shape == (count, depth)
            else pl.BlockSpec(
                (pl.Element(count), pl.Element(depth)),
                lambda i, core_ref: (first, pl.multiple_of(core_ref[0] * depth, LANES)),
                pipeline_mode=pl.Buffered(1),
            ),
            fixed((count, depth)),
            pl.BlockSpec((depth, tile), lambda i, *_: (0, low // tile + i)),
        ],
        out_specs,
        out_shape,
        grid=(steps,),
        scalars=core,
    )(features, other_rows, up_weight)
    parts = [results[n:m] for n, m in zip(firsts[:-1], firsts[1:])]
    return [(part[0], part[1:]) for part in parts], mark


def _gcd(x, y):
    while y:
        x, y = y, x % y
    return x


def add_parts(own, messages, tile, after):
    count, total = own.shape
    where, _ = in_messages(total // tile, tile, len(messages))

    def body(scalar_ref, inputs, outputs, scratch):
        for step, parts in enumerate(where):

            @pl.when(pl.program_id(0) == step)
            def _(parts=parts):
                other = from_messages(inputs[1:], parts).astype(F32)
                outputs[0][...] = (inputs[0][...].astype(F32) + other).astype(BF16)

    tile_spec = pl.BlockSpec((count, tile), lambda i, *_: (0, i))
    return ordered(
        "add",
        body,
        after,
        [tile_spec] + [fixed(part.shape) for part in messages],
        [tile_spec],
        [jax.ShapeDtypeStruct((count, total), BF16)],
        grid=(total // tile,),
        vmem=SMALL_VMEM_BYTES,
    )(own, *messages)


def gate(array, after):
    def body(scalar_ref, inputs, outputs, scratch):
        pass

    spec = pl.BlockSpec(memory_space=pl.ANY)
    return ordered(
        "gate",
        body,
        after,
        [spec],
        [spec],
        [jax.ShapeDtypeStruct(array.shape, array.dtype)],
        vmem=SMALL_VMEM_BYTES,
        aliases=((0, 0),),
    )(array)


def slope_rows(mine, theirs, out_grad, tokens, span, tile, number, after):
    (start_row, end_row), (low, high) = tokens, span
    count = end_row - start_row
    where, widths = in_messages((high - low) // tile, tile, number)

    def body(scalar_ref, inputs, outputs, scratch):
        preact = inputs[0][...].astype(F32) + inputs[1][...].astype(F32)
        sigmoid_value = 0.5 * jnp.tanh(0.5 * preact) + 0.5
        rows = (
            inputs[2][...].astype(F32) * sigmoid_value * (1.0 + preact * (1.0 - sigmoid_value))
        ).astype(BF16)
        for step, parts in enumerate(where):

            @pl.when(pl.program_id(0) == step)
            def _(parts=parts):
                to_messages(outputs, parts, rows)

    tile_spec = pl.BlockSpec((count, tile), lambda i, *_: (0, i))
    *results, mark = ordered(
        "slope",
        body,
        after,
        [
            tile_spec,
            tile_spec,
            pl.BlockSpec(
                (pl.Element(count), pl.Element(tile)),
                lambda i, *_: (start_row, pl.multiple_of(low + i * tile, LANES)),
            ),
        ],
        [pl.BlockSpec((count, width), lambda i, *_: (0, 0)) for width in widths],
        [jax.ShapeDtypeStruct((count, width), BF16) for width in widths],
        grid=((high - low) // tile,),
        vmem=SMALL_VMEM_BYTES,
    )(mine, theirs, out_grad)
    return results, mark


def backward(own_messages, other_messages, span, tile, up_weight, left_rows, total, place, blocks, last, after):
    low = span[0]
    depth = up_weight.shape[0]
    count = own_messages[0].shape[0]
    width = depth // blocks
    parts = 2 * blocks
    steps = (span[1] - low) // tile
    where, widths = in_messages(steps, tile, len(own_messages))
    messages = len(widths)

    def body(scalar_ref, inputs, outputs, scratch):
        step = pl.program_id(0)
        weight, left = inputs[:2]
        own_refs, other_refs = inputs[2 : 2 + messages], inputs[2 + messages : 2 + 2 * messages]
        sums, left_sums = scratch if last else outputs

        @pl.when(step == 0)
        def _():
            if total is None:
                sums[...] = jnp.zeros_like(sums)
                left_sums[...] = jnp.zeros_like(left_sums)
            else:
                sums[...] = inputs[-2][...]
                left_sums[...] = inputs[-1][...]

        for n, places in enumerate(where):

            @pl.when(step == n)
            def _(places=places):
                own = from_messages(own_refs, places)
                both = jnp.concatenate([own, from_messages(other_refs, places)], axis=0)
                for block in range(blocks):
                    product = contract_last(both, weight[block * width : (block + 1) * width, :])
                    sums[2 * block] += product[:count]
                    sums[2 * block + 1] += product[count:]
                left_sums[...] += contract_last(own, left[...])

        if last:

            @pl.when(step == steps - 1)
            def _():
                for n in range(blocks):
                    block = lax.rem(scalar_ref[0] + n, blocks)
                    for r in range(2):
                        held = scalar_ref[1] if r == 0 else 1 - scalar_ref[1]
                        at = pl.multiple_of(held * count, 16)
                        outputs[n][pl.ds(at, count), :] = sums[2 * block + r].astype(BF16)
                outputs[blocks][...] = left_sums[...]

    sums_shape, left_shape = (parts, count, width), (count, left_rows.shape[0])
    sums_spec = pl.BlockSpec(sums_shape, lambda i, *_: (0, 0, 0))
    left_spec = pl.BlockSpec(left_shape, lambda i, *_: (0, 0))
    in_specs = [
        pl.BlockSpec((depth, tile), lambda i, *_: (0, low // tile + i)),
        pl.BlockSpec((left_rows.shape[0], tile), lambda i, *_: (0, low // tile + i)),
    ]
    operands = [up_weight, left_rows, *own_messages, *other_messages]
    in_specs += [fixed((count, size)) for size in widths] * 2
    if total is not None:
        in_specs += [fixed(sums_shape), fixed(left_shape)]
        operands += total
    if last:
        out_specs = [pl.BlockSpec((2 * count, width), lambda i, *_: (0, 0))] * blocks + [left_spec]
        out_shape = [jax.ShapeDtypeStruct((2 * count, width), BF16)] * blocks
        out_shape.append(jax.ShapeDtypeStruct(left_shape, F32))
        scratch = [pltpu.VMEM(sums_shape, F32), pltpu.VMEM(left_shape, F32)]
    else:
        out_specs = [sums_spec, left_spec]
        out_shape = [jax.ShapeDtypeStruct(sums_shape, F32), jax.ShapeDtypeStruct(left_shape, F32)]
        scratch = []
    *results, mark = ordered(
        "backward", body, after, in_specs, out_specs, out_shape, (steps,), scratch, place
    )(*operands)
    return results, mark


def exchange(message, n, blocks):
    pairs = []
    for t in range(lax.axis_size("tensor")):
        for c in range(2):
            pairs.append((2 * t + c, 2 * (blocks * c + (t + n) % blocks) + t // blocks))
    return lax.ppermute(message, ("tensor", "dp"), pairs)


def gathered_sum(arrived, core, after):
    count, width = arrived[0].shape[0] // 2, arrived[0].shape[1]

    def body(scalar_ref, inputs, outputs, scratch):
        for output, held in zip(outputs, (scalar_ref[0], 1 - scalar_ref[0])):
            rows = pl.ds(pl.multiple_of(held * count, 16), count)
            output[...] = sum(ref[rows, :].astype(F32) for ref in inputs).astype(output.dtype)

    spec = pl.BlockSpec((count, width), lambda i, *_: (0, 0))
    own, message, mark = ordered(
        "gathered_sum",
        body,
        after,
        [pl.BlockSpec(array.shape, lambda i, *_: (0, 0)) for array in arrived],
        [spec, spec],
        [jax.ShapeDtypeStruct((count, width), F32), jax.ShapeDtypeStruct((count, width), BF16)],
        scalars=core,
    )(*arrived)
    return own, lax.ppermute(message, "dp", [(0, 1), (1, 0)]), mark


def paired(features, up_weight, out_grad, left_factors, right_factors, token_ids, query_ids):
    query_count, rank_count = left_factors.shape[:2]
    left_rows = left_factors.reshape(query_count * rank_count, left_factors.shape[2])
    right_rows = right_factors.reshape(query_count * rank_count, right_factors.shape[2])
    token_count, hidden = out_grad.shape
    depth = up_weight.shape[0]
    blocks = lax.axis_size("tensor") // 2
    core = lax.axis_index("dp")
    swap = [(0, 1), (1, 0)]
    place = jnp.stack([lax.rem(lax.axis_index("tensor"), blocks), core]).astype(jnp.int32)

    tokens = cuts(token_count, 16, TOKEN_SHARES)
    groups = [(tokens[:1], cuts(hidden, LANES, HEAD_SHARES)), (tokens[1:], cuts(hidden, LANES, REST_SHARES))]

    core_ref = core.astype(jnp.int32).reshape(1)
    mark = jnp.zeros((8, LANES), F32)
    from_other, adds, mine, theirs, rows = {}, {}, {}, {}, {}
    totals, held, arrived, lefts, results = {}, {}, {}, {}, {}

    def run_half(g, mark):
        span = (groups[g][0][0][0], groups[g][0][-1][1])
        away, mark = half_of(features, span, depth, core_ref, [mark])
        from_other[g] = lax.ppermute(away, "dp", swap)
        return mark

    low, high = tokens[0]
    first_own = lax.dynamic_slice(features, (low, core * depth), (high - low, depth))
    first_away = lax.dynamic_slice(features, (low, (1 - core) * depth), (high - low, depth))

    def run_forward(g, j, mark):
        token_spans, spans = groups[g]
        first = 0 if g == 0 else 1
        numbers = [FORWARD_MESSAGES[first + t][j] for t in range(len(token_spans))]
        results, mark = forward(
            features if g else first_own, from_other[g], up_weight, core_ref, spans[j], token_spans, numbers, [mark]
        )
        for t, (own, send) in enumerate(results):
            adds[first + t, j] = (own, [lax.ppermute(part, "dp", swap) for part in send])
        return mark

    def span_of(piece):
        return groups[min(piece[0], 1)][1][piece[1]]

    def tile_for(piece):
        low, high = span_of(piece)
        return tile_of(_gcd(high - low, low), 1024)

    def run_add(piece, mark, *after):
        own, messages = adds[piece]
        held_back = piece == (0, 1)
        mine[piece], mark = add_parts(
            own, messages, tile_for(piece), [mark] if held_back else [mark, *after]
        )
        if held_back:
            mine[piece], mark = gate(mine[piece], [mark, *after])
        theirs[piece] = lax.ppermute(mine[piece], "query", swap)
        return mark

    def run_slope(piece, mark, *after):
        own, mark = slope_rows(
            mine[piece],
            theirs[piece],
            out_grad,
            tokens[piece[0]],
            span_of(piece),
            tile_for(piece),
            SLOPE_MESSAGES[piece[0]][piece[1]],
            [mark, *after],
        )
        rows[piece] = (own, [lax.ppermute(part, "dp", swap) for part in own])
        return mark

    def run_backward(piece, last, mark, *after):
        t = piece[0]
        results, mark = backward(
            *rows[piece],
            span_of(piece),
            tile_for(piece),
            up_weight,
            left_rows,
            totals.get(t),
            place,
            blocks,
            last,
            [mark, *after],
        )
        if last:
            held[t], lefts[t] = results[:-1], results[-1]
        else:
            totals[t] = results
        return mark

    def send_sums(t):
        arrived[t] = [exchange(part, n, blocks) for n, part in enumerate(held[t])]

    def add_sums(t, mark):
        own, other, mark = gathered_sum(arrived[t], core_ref, [mark])
        results[t] = (own + other.astype(F32)).astype(BF16)
        return mark

    tensor_size = lax.axis_size("tensor")
    tensor_index = lax.axis_index("tensor")
    fold = tensor_size // 2
    owns = (tensor_index // fold == lax.axis_index("query")).astype(jnp.int32).reshape(1)
    where = jnp.stack([core, tensor_index % fold * right_rows.shape[1]]).astype(jnp.int32)
    back = [(b, a) for a, b in right_pairs(tensor_size)]

    def across(array, step):
        return lax.ppermute(array, "tensor", [(t, t ^ step) for t in range(tensor_size)])

    from_other[0] = lax.ppermute(first_away, "dp", swap)
    right_here = right_send(right_rows)
    mark = run_forward(0, 0, mark)
    mark = run_add((0, 0), mark, right_here)
    mark = run_forward(0, 1, mark)
    right_there = lax.ppermute(right_here, "dp", swap)
    mark = run_half(1, mark)
    right_own, for_other, mark = right_products(
        features, right_rows, right_here, right_there, where, [mark]
    )
    received = lax.ppermute(for_other, ("tensor", "query"), back)
    mark = run_add((0, 1), mark, theirs[0, 0], received)
    mark = run_slope((0, 0), mark)
    mark = run_forward(1, 0, mark)
    right_part, mark = right_choice(right_own, received, owns, [mark])
    right_other = across(right_part, 1)
    mark = run_add((1, 0), mark)
    mark = run_forward(1, 1, mark)
    mark = run_slope((0, 1), mark)
    mark = run_add((1, 1), mark)
    mark = run_backward((0, 0), False, mark)
    right_sum = right_part
    for step in range(1, tensor_size.bit_length() - 1):
        right_sum, message, mark = add_right(right_sum, right_other, [mark])
        right_other = across(message, 1 << step)
    mark = run_backward((0, 1), True, mark, *adds[2, 0][1])
    send_sums(0)
    mark = run_slope((1, 0), mark, right_other)
    mark = run_backward((1, 0), False, mark)
    mark = run_add((2, 0), mark)
    mark = run_slope((1, 1), mark, arrived[0][0])
    mark = run_backward((1, 1), True, mark)
    send_sums(1)
    mark = run_add((2, 1), mark)
    mark = add_sums(0, mark)
    mark = run_slope((2, 0), mark)
    mark = run_backward((2, 0), False, mark)
    mark = run_slope((2, 1), mark, arrived[1][0])
    mark = run_backward((2, 1), True, mark)
    send_sums(2)
    mark = add_sums(1, mark)
    mark = add_sums(2, mark)

    right_sum = right_sum.astype(F32) + right_other.astype(F32)
    weighted, grads = 0.0, []
    for t, (low, high) in enumerate(tokens):
        membership = (
            token_ids[None, low:high] == jnp.arange(EXAMPLES, dtype=jnp.int32)[:, None]
        ).astype(F32)
        weighted = weighted + exact_dot(membership, lefts[t] * right_sum[low:high])
        grads.append(results[t])
    choice = column_choice(query_ids, query_count, rank_count)
    scores = lax.psum(exact_dot(weighted, choice) / rank_count, ("tensor", "dp"))
    return jnp.concatenate(grads, axis=0), scores


def broadcast(value, axis, source):
    kept = jnp.where(lax.axis_index(axis) == source, value, 0).astype(value.dtype)
    return lax.psum(kept, axis)


def general(features, up_weight, out_grad, left_factors, right_factors, token_ids, query_ids):
    query_count, rank_count = left_factors.shape[:2]
    local_rows = lax.all_gather(up_weight, "dp", axis=0, tiled=True)
    preact_part = jnp.dot(features, local_rows, preferred_element_type=jnp.float32)
    preact_share = lax.psum_scatter(preact_part, "query", scatter_dimension=0, tiled=True)
    share_rows = preact_share.shape[0]
    own_grad = lax.dynamic_slice_in_dim(
        out_grad, lax.axis_index("query") * share_rows, share_rows, 0
    )
    grad_rows = lax.all_gather(silu_slope(preact_share, own_grad), "query", axis=0, tiled=True)
    input_part = contract_last(grad_rows, local_rows)
    input_grad = lax.psum_scatter(input_part, "tensor", scatter_dimension=1, tiled=True).astype(
        jnp.bfloat16
    )
    fold_ratio = lax.axis_size("tensor") // lax.axis_size("query")
    tensor_index = lax.axis_index("tensor")
    block_width = right_factors.shape[2]
    feature_piece = lax.dynamic_slice_in_dim(
        features, tensor_index % fold_ratio * block_width, block_width, 1
    )
    feature_block = broadcast(feature_piece, "query", tensor_index // fold_ratio)
    left_proj = contract_last(
        grad_rows, left_factors.reshape(query_count * rank_count, left_factors.shape[2])
    )
    right_proj = contract_last(
        feature_block, right_factors.reshape(query_count * rank_count, block_width)
    )
    left_sum, right_sum = lax.psum((left_proj, right_proj), "tensor")
    membership = (token_ids[None, :] == jnp.arange(EXAMPLES, dtype=jnp.int32)[:, None]).astype(
        jnp.float32
    )
    weighted = exact_dot(membership, left_sum * right_sum)
    choice = column_choice(query_ids, query_count, rank_count)
    scores = lax.psum(exact_dot(weighted, choice) / rank_count, "dp")
    return (input_grad, scores)


def solution(mesh):
    size = mesh.shape
    is_paired = size["query"] == 2 and size["dp"] == 2 and size["tensor"] in (2, 4, 8, 16)
    return jax.shard_map(
        paired if is_paired else general,
        mesh=mesh,
        in_specs=(
            P(("groups", "dp"), "query"),
            P(("query", "dp"), "tensor"),
            P(("groups", "dp"), "tensor"),
            P("query", None, "tensor"),
            P("query", None, "tensor"),
            P(("groups", "dp")),
            P("query", None),
        ),
        out_specs=(P(("groups", "dp"), ("query", "tensor")), P("groups", "query")),
        check_vma=False,
    )
```

```python
import jax
import jax.numpy as jnp
from jax import lax
from jax.experimental import pallas as pl
from jax.experimental.pallas import tpu as pltpu
from jax.sharding import PartitionSpec as P

EXAMPLES = 16
LANES = 128
TOKEN_SHARES = (13, 12, 7)
HEAD_SHARES = (3, 4)
REST_SHARES = (4, 3)
FORWARD_MESSAGES = ((3, 2), (3, 2), (1, 1))
SLOPE_MESSAGES = ((2, 2), (3, 2), (2, 2))
VMEM_BYTES = 24 << 20
SMALL_VMEM_BYTES = 12 << 20
F32, BF16 = jnp.float32, jnp.bfloat16


def silu_slope(preact, grad_part):
    sigmoid_value = jax.nn.sigmoid(preact)
    return (
        grad_part.astype(jnp.float32) * sigmoid_value * (1.0 + preact * (1.0 - sigmoid_value))
    ).astype(jnp.bfloat16)


def contract_last(left_rows, right_rows):
    return lax.dot_general(
        left_rows, right_rows, (((1,), (1,)), ((), ())), preferred_element_type=jnp.float32
    )


def cuts(total, unit, shares):
    whole, marks, seen = sum(shares), [0], 0
    for share in shares:
        seen += share
        mark = total * seen // whole // unit * unit if seen < whole else total
        if mark > marks[-1]:
            marks.append(mark)
    return list(zip(marks[:-1], marks[1:]))


def column_choice(query_ids, query_count, rank_count):
    owner = jnp.arange(query_count * rank_count, dtype=jnp.int32) // rank_count
    return (owner[:, None] == query_ids[0][None, :]).astype(jnp.float32)


def exact_dot(a, b):
    return jnp.dot(a, b, precision=lax.Precision.HIGHEST, preferred_element_type=jnp.float32)


def right_pairs(tensor_size):
    fold = tensor_size // 2
    return [(2 * t + 1 - t // fold, 2 * t + t // fold) for t in range(tensor_size)]


def right_send(right_rows):
    half = right_rows.shape[0] // 2
    piece = lax.dynamic_slice_in_dim(right_rows, lax.axis_index("dp") * half, half, 0)
    return lax.ppermute(piece, ("tensor", "query"), right_pairs(lax.axis_size("tensor")))


def right_products(features, right_rows, here, there, where, after):
    rows, depth = right_rows.shape
    half = rows // 2
    count = features.shape[0]

    def body(scalar_ref, inputs, outputs, scratch):
        block = inputs[0][...]
        outputs[0][...] = contract_last(block, inputs[1][...])
        first, second = contract_last(block, inputs[2][...]), contract_last(block, inputs[3][...])
        is_first = scalar_ref[0] == 0
        outputs[1][:, :half] = jnp.where(is_first, first, second).astype(BF16)
        outputs[1][:, half:] = jnp.where(is_first, second, first).astype(BF16)

    whole = pl.BlockSpec((count, rows), lambda i, *_: (0, 0))
    own, for_other, mark = ordered(
        "right",
        body,
        after,
        [
            pl.BlockSpec(
                (pl.Element(count), pl.Element(depth)),
                lambda i, where_ref: (0, pl.multiple_of(where_ref[1], LANES)),
            ),
            pl.BlockSpec((rows, depth), lambda i, *_: (0, 0)),
            pl.BlockSpec((half, depth), lambda i, *_: (0, 0)),
            pl.BlockSpec((half, depth), lambda i, *_: (0, 0)),
        ],
        [whole, whole],
        [jax.ShapeDtypeStruct((count, rows), F32), jax.ShapeDtypeStruct((count, rows), BF16)],
        scalars=where,
    )(features, right_rows, here, there)
    return own, for_other, mark


def right_choice(own, received, owns, after):
    def body(scalar_ref, inputs, outputs, scratch):
        outputs[0][...] = jnp.where(
            scalar_ref[0] == 1, inputs[0][...], inputs[1][...].astype(F32)
        ).astype(BF16)

    whole = pl.BlockSpec(own.shape, lambda i, *_: (0, 0))
    return ordered(
        "right_choice",
        body,
        after,
        [whole, whole],
        [whole],
        [jax.ShapeDtypeStruct(own.shape, BF16)],
        scalars=owns,
        vmem=SMALL_VMEM_BYTES,
    )(own, received)


def tile_of(width, limit):
    return max(t for t in range(LANES, limit + 1, LANES) if width % t == 0)


def fixed(shape):
    return pl.BlockSpec(shape, lambda i, *_: (0,) * len(shape), pipeline_mode=pl.Buffered(1))


def ordered(name, body, after, in_specs, out_specs, out_shape, grid=(1,), scratch_shapes=(), scalars=None, vmem=VMEM_BYTES, aliases=()):
    def kernel(scalar_ref, *refs):
        refs = refs[len(after) :]
        inputs, rest = refs[: len(in_specs)], refs[len(in_specs) :]
        outputs, own_mark, scratch = (
            rest[: len(out_specs)],
            rest[len(out_specs)],
            rest[len(out_specs) + 1 :],
        )
        own_mark[...] = jnp.zeros_like(own_mark)
        body(scalar_ref, inputs, outputs, scratch)

    mark_spec = pl.BlockSpec((8, LANES), lambda *ids: (0, 0))

    if scalars is None:
        scalars = jnp.zeros((1,), jnp.int32)

    def call(*operands):
        return pl.pallas_call(
            kernel,
            grid_spec=pltpu.PrefetchScalarGridSpec(
                num_scalar_prefetch=1,
                grid=grid,
                in_specs=[pl.BlockSpec(memory_space=pl.ANY)] * len(after) + list(in_specs),
                out_specs=list(out_specs) + [mark_spec],
                scratch_shapes=list(scratch_shapes),
            ),
            out_shape=list(out_shape) + [jax.ShapeDtypeStruct((8, LANES), F32)],
            compiler_params=pltpu.CompilerParams(vmem_limit_bytes=vmem),
            cost_estimate=pl.CostEstimate(flops=1, bytes_accessed=1, transcendentals=0),
            name=name,
            input_output_aliases={1 + len(after) + source: target for source, target in aliases},
        )(scalars, *after, *operands)

    return call


def half_of(features, tokens, depth, core, after):
    low, high = tokens

    def body(scalar_ref, inputs, outputs, scratch):
        outputs[0][...] = inputs[0][...]

    return ordered(
        "half",
        body,
        after,
        [
            pl.BlockSpec(
                (pl.Element(high - low), pl.Element(depth)),
                lambda i, core_ref: (low, pl.multiple_of((1 - core_ref[0]) * depth, LANES)),
            )
        ],
        [pl.BlockSpec((high - low, depth), lambda i, *_: (0, 0))],
        [jax.ShapeDtypeStruct((high - low, depth), features.dtype)],
        scalars=core,
        vmem=SMALL_VMEM_BYTES,
    )(features)


def add_right(own, received, after):
    def body(scalar_ref, inputs, outputs, scratch):
        total = inputs[0][...].astype(F32) + inputs[1][...].astype(F32)
        outputs[0][...] = total
        outputs[1][...] = total.astype(BF16)

    whole = pl.BlockSpec(own.shape, lambda i, *_: (0, 0))
    total, message, mark = ordered(
        "add_right",
        body,
        after,
        [whole, whole],
        [whole, whole],
        [jax.ShapeDtypeStruct(own.shape, F32), jax.ShapeDtypeStruct(own.shape, BF16)],
        vmem=SMALL_VMEM_BYTES,
    )(own, received)
    return total, message, mark


def in_messages(steps, tile, number):
    marks = cuts(steps * tile, LANES, (1,) * number)
    where = []
    for step in range(steps):
        parts = []
        for message, (low, high) in enumerate(marks):
            begin, end = max(low, step * tile), min(high, (step + 1) * tile)
            if begin < end:
                parts.append((message, begin - low, begin - step * tile, end - begin))
        where.append(parts)
    return where, [high - low for low, high in marks]


def from_messages(refs, parts):
    found = [refs[message][:, at : at + size] for message, at, _, size in parts]
    return found[0] if len(found) == 1 else jnp.concatenate(found, axis=1)


def to_messages(refs, parts, value):
    for message, at, begin, size in parts:
        refs[message][:, at : at + size] = value[:, begin : begin + size]


def forward(features, other_rows, up_weight, core, span, spans_of_tokens, numbers, after):
    low, high = span
    depth = up_weight.shape[0]
    tile = tile_of(_gcd(high - low, low), 1024)
    steps = (high - low) // tile
    count = other_rows.shape[0]
    first = spans_of_tokens[0][0]
    plans = [in_messages(steps, tile, number) for number in numbers]
    firsts = [0]
    for _, widths in plans:
        firsts.append(firsts[-1] + 1 + len(widths))

    def body(scalar_ref, inputs, outputs, scratch):
        rows = jnp.concatenate([inputs[0][...], inputs[1][...]], axis=0)
        product = jnp.dot(rows, inputs[2][...], preferred_element_type=F32)
        for n, (a, b) in enumerate(spans_of_tokens):
            outputs[firsts[n]][...] = product[a - first : b - first].astype(BF16)
            send = product[count + a - first : count + b - first].astype(BF16)
            for step, parts in enumerate(plans[n][0]):

                @pl.when(pl.program_id(0) == step)
                def _(send=send, n=n, parts=parts):
                    to_messages(outputs[firsts[n] + 1 :], parts, send)

    out_specs, out_shape = [], []
    for (a, b), (_, widths) in zip(spans_of_tokens, plans):
        out_specs.append(pl.BlockSpec((b - a, tile), lambda i, *_: (0, i)))
        out_shape.append(jax.ShapeDtypeStruct((b - a, high - low), BF16))
        out_specs += [pl.BlockSpec((b - a, width), lambda i, *_: (0, 0)) for width in widths]
        out_shape += [jax.ShapeDtypeStruct((b - a, width), BF16) for width in widths]
    *results, mark = ordered(
        "forward",
        body,
        after,
        [
            fixed((count, depth))
            if features.shape == (count, depth)
            else pl.BlockSpec(
                (pl.Element(count), pl.Element(depth)),
                lambda i, core_ref: (first, pl.multiple_of(core_ref[0] * depth, LANES)),
                pipeline_mode=pl.Buffered(1),
            ),
            fixed((count, depth)),
            pl.BlockSpec((depth, tile), lambda i, *_: (0, low // tile + i)),
        ],
        out_specs,
        out_shape,
        grid=(steps,),
        scalars=core,
    )(features, other_rows, up_weight)
    parts = [results[n:m] for n, m in zip(firsts[:-1], firsts[1:])]
    return [(part[0], part[1:]) for part in parts], mark


def _gcd(x, y):
    while y:
        x, y = y, x % y
    return x


def add_parts(own, messages, tile, after):
    count, total = own.shape
    where, _ = in_messages(total // tile, tile, len(messages))

    def body(scalar_ref, inputs, outputs, scratch):
        for step, parts in enumerate(where):

            @pl.when(pl.program_id(0) == step)
            def _(parts=parts):
                other = from_messages(inputs[1:], parts).astype(F32)
                outputs[0][...] = (inputs[0][...].astype(F32) + other).astype(BF16)

    tile_spec = pl.BlockSpec((count, tile), lambda i, *_: (0, i))
    return ordered(
        "add",
        body,
        after,
        [tile_spec] + [fixed(part.shape) for part in messages],
        [tile_spec],
        [jax.ShapeDtypeStruct((count, total), BF16)],
        grid=(total // tile,),
        vmem=SMALL_VMEM_BYTES,
    )(own, *messages)


def gate(array, after):
    def body(scalar_ref, inputs, outputs, scratch):
        pass

    spec = pl.BlockSpec(memory_space=pl.ANY)
    return ordered(
        "gate",
        body,
        after,
        [spec],
        [spec],
        [jax.ShapeDtypeStruct(array.shape, array.dtype)],
        vmem=SMALL_VMEM_BYTES,
        aliases=((0, 0),),
    )(array)


def slope_rows(mine, theirs, out_grad, tokens, span, tile, number, after):
    (start_row, end_row), (low, high) = tokens, span
    count = end_row - start_row
    where, widths = in_messages((high - low) // tile, tile, number)

    def body(scalar_ref, inputs, outputs, scratch):
        preact = inputs[0][...].astype(F32) + inputs[1][...].astype(F32)
        sigmoid_value = 0.5 * jnp.tanh(0.5 * preact) + 0.5
        rows = (
            inputs[2][...].astype(F32) * sigmoid_value * (1.0 + preact * (1.0 - sigmoid_value))
        ).astype(BF16)
        for step, parts in enumerate(where):

            @pl.when(pl.program_id(0) == step)
            def _(parts=parts):
                to_messages(outputs, parts, rows)

    tile_spec = pl.BlockSpec((count, tile), lambda i, *_: (0, i))
    *results, mark = ordered(
        "slope",
        body,
        after,
        [
            tile_spec,
            tile_spec,
            pl.BlockSpec(
                (pl.Element(count), pl.Element(tile)),
                lambda i, *_: (start_row, pl.multiple_of(low + i * tile, LANES)),
            ),
        ],
        [pl.BlockSpec((count, width), lambda i, *_: (0, 0)) for width in widths],
        [jax.ShapeDtypeStruct((count, width), BF16) for width in widths],
        grid=((high - low) // tile,),
        vmem=SMALL_VMEM_BYTES,
    )(mine, theirs, out_grad)
    return results, mark


def backward(own_messages, other_messages, span, tile, up_weight, left_rows, total, place, blocks, last, after):
    low = span[0]
    depth = up_weight.shape[0]
    count = own_messages[0].shape[0]
    width = depth // blocks
    parts = 2 * blocks
    steps = (span[1] - low) // tile
    where, widths = in_messages(steps, tile, len(own_messages))
    messages = len(widths)

    def body(scalar_ref, inputs, outputs, scratch):
        step = pl.program_id(0)
        weight, left = inputs[:2]
        own_refs, other_refs = inputs[2 : 2 + messages], inputs[2 + messages : 2 + 2 * messages]
        sums, left_sums = scratch if last else outputs

        @pl.when(step == 0)
        def _():
            if total is None:
                sums[...] = jnp.zeros_like(sums)
                left_sums[...] = jnp.zeros_like(left_sums)
            else:
                sums[...] = inputs[-2][...]
                left_sums[...] = inputs[-1][...]

        for n, places in enumerate(where):

            @pl.when(step == n)
            def _(places=places):
                own = from_messages(own_refs, places)
                both = jnp.concatenate([own, from_messages(other_refs, places)], axis=0)
                for block in range(blocks):
                    product = contract_last(both, weight[block * width : (block + 1) * width, :])
                    sums[2 * block] += product[:count]
                    sums[2 * block + 1] += product[count:]
                left_sums[...] += contract_last(own, left[...])

        if last:

            @pl.when(step == steps - 1)
            def _():
                for n in range(blocks):
                    block = lax.rem(scalar_ref[0] + n, blocks)
                    for r in range(2):
                        held = scalar_ref[1] if r == 0 else 1 - scalar_ref[1]
                        at = pl.multiple_of(held * count, 16)
                        outputs[n][pl.ds(at, count), :] = sums[2 * block + r].astype(BF16)
                outputs[blocks][...] = left_sums[...]

    sums_shape, left_shape = (parts, count, width), (count, left_rows.shape[0])
    sums_spec = pl.BlockSpec(sums_shape, lambda i, *_: (0, 0, 0))
    left_spec = pl.BlockSpec(left_shape, lambda i, *_: (0, 0))
    in_specs = [
        pl.BlockSpec((depth, tile), lambda i, *_: (0, low // tile + i)),
        pl.BlockSpec((left_rows.shape[0], tile), lambda i, *_: (0, low // tile + i)),
    ]
    operands = [up_weight, left_rows, *own_messages, *other_messages]
    in_specs += [fixed((count, size)) for size in widths] * 2
    if total is not None:
        in_specs += [fixed(sums_shape), fixed(left_shape)]
        operands += total
    if last:
        out_specs = [pl.BlockSpec((2 * count, width), lambda i, *_: (0, 0))] * blocks + [left_spec]
        out_shape = [jax.ShapeDtypeStruct((2 * count, width), BF16)] * blocks
        out_shape.append(jax.ShapeDtypeStruct(left_shape, F32))
        scratch = [pltpu.VMEM(sums_shape, F32), pltpu.VMEM(left_shape, F32)]
    else:
        out_specs = [sums_spec, left_spec]
        out_shape = [jax.ShapeDtypeStruct(sums_shape, F32), jax.ShapeDtypeStruct(left_shape, F32)]
        scratch = []
    *results, mark = ordered(
        "backward", body, after, in_specs, out_specs, out_shape, (steps,), scratch, place
    )(*operands)
    return results, mark


def exchange(message, n, blocks):
    pairs = []
    for t in range(lax.axis_size("tensor")):
        for c in range(2):
            pairs.append((2 * t + c, 2 * (blocks * c + (t + n) % blocks) + t // blocks))
    return lax.ppermute(message, ("tensor", "dp"), pairs)


def gathered_sum(arrived, core, after):
    count, width = arrived[0].shape[0] // 2, arrived[0].shape[1]

    def body(scalar_ref, inputs, outputs, scratch):
        for output, held in zip(outputs, (scalar_ref[0], 1 - scalar_ref[0])):
            rows = pl.ds(pl.multiple_of(held * count, 16), count)
            output[...] = sum(ref[rows, :].astype(F32) for ref in inputs).astype(output.dtype)

    spec = pl.BlockSpec((count, width), lambda i, *_: (0, 0))
    own, message, mark = ordered(
        "gathered_sum",
        body,
        after,
        [pl.BlockSpec(array.shape, lambda i, *_: (0, 0)) for array in arrived],
        [spec, spec],
        [jax.ShapeDtypeStruct((count, width), F32), jax.ShapeDtypeStruct((count, width), BF16)],
        scalars=core,
    )(*arrived)
    return own, lax.ppermute(message, "dp", [(0, 1), (1, 0)]), mark


def paired(features, up_weight, out_grad, left_factors, right_factors, token_ids, query_ids):
    query_count, rank_count = left_factors.shape[:2]
    left_rows = left_factors.reshape(query_count * rank_count, left_factors.shape[2])
    right_rows = right_factors.reshape(query_count * rank_count, right_factors.shape[2])
    token_count, hidden = out_grad.shape
    depth = up_weight.shape[0]
    blocks = lax.axis_size("tensor") // 2
    core = lax.axis_index("dp")
    swap = [(0, 1), (1, 0)]
    place = jnp.stack([lax.rem(lax.axis_index("tensor"), blocks), core]).astype(jnp.int32)

    tokens = cuts(token_count, 16, TOKEN_SHARES)
    groups = [(tokens[:1], cuts(hidden, LANES, HEAD_SHARES)), (tokens[1:], cuts(hidden, LANES, REST_SHARES))]

    core_ref = core.astype(jnp.int32).reshape(1)
    mark = jnp.zeros((8, LANES), F32)
    from_other, adds, mine, theirs, rows = {}, {}, {}, {}, {}
    totals, held, arrived, lefts, results = {}, {}, {}, {}, {}

    def run_half(g, mark):
        span = (groups[g][0][0][0], groups[g][0][-1][1])
        away, mark = half_of(features, span, depth, core_ref, [mark])
        from_other[g] = lax.ppermute(away, "dp", swap)
        return mark

    low, high = tokens[0]
    first_own = lax.dynamic_slice(features, (low, core * depth), (high - low, depth))
    first_away = lax.dynamic_slice(features, (low, (1 - core) * depth), (high - low, depth))

    def run_forward(g, j, mark):
        token_spans, spans = groups[g]
        first = 0 if g == 0 else 1
        numbers = [FORWARD_MESSAGES[first + t][j] for t in range(len(token_spans))]
        results, mark = forward(
            features if g else first_own, from_other[g], up_weight, core_ref, spans[j], token_spans, numbers, [mark]
        )
        for t, (own, send) in enumerate(results):
            adds[first + t, j] = (own, [lax.ppermute(part, "dp", swap) for part in send])
        return mark

    def span_of(piece):
        return groups[min(piece[0], 1)][1][piece[1]]

    def tile_for(piece):
        low, high = span_of(piece)
        return tile_of(_gcd(high - low, low), 1024)

    def run_add(piece, mark, *after):
        own, messages = adds[piece]
        mine[piece], mark = add_parts(own, messages, tile_for(piece), [mark])
        if after:
            mine[piece], mark = gate(mine[piece], [mark, *after])
        theirs[piece] = lax.ppermute(mine[piece], "query", swap)
        return mark

    def run_slope(piece, mark, *after):
        own, mark = slope_rows(
            mine[piece],
            theirs[piece],
            out_grad,
            tokens[piece[0]],
            span_of(piece),
            tile_for(piece),
            SLOPE_MESSAGES[piece[0]][piece[1]],
            [mark, *after],
        )
        rows[piece] = (own, [lax.ppermute(part, "dp", swap) for part in own])
        return mark

    def run_backward(piece, last, mark, *after):
        t = piece[0]
        results, mark = backward(
            *rows[piece],
            span_of(piece),
            tile_for(piece),
            up_weight,
            left_rows,
            totals.get(t),
            place,
            blocks,
            last,
            [mark, *after],
        )
        if last:
            held[t], lefts[t] = results[:-1], results[-1]
        else:
            totals[t] = results
        return mark

    def send_sums(t):
        arrived[t] = [exchange(part, n, blocks) for n, part in enumerate(held[t])]

    def add_sums(t, mark):
        own, other, mark = gathered_sum(arrived[t], core_ref, [mark])
        results[t] = (own + other.astype(F32)).astype(BF16)
        return mark

    tensor_size = lax.axis_size("tensor")
    tensor_index = lax.axis_index("tensor")
    fold = tensor_size // 2
    owns = (tensor_index // fold == lax.axis_index("query")).astype(jnp.int32).reshape(1)
    where = jnp.stack([core, tensor_index % fold * right_rows.shape[1]]).astype(jnp.int32)
    back = [(b, a) for a, b in right_pairs(tensor_size)]

    def across(array, step):
        return lax.ppermute(array, "tensor", [(t, t ^ step) for t in range(tensor_size)])

    from_other[0] = lax.ppermute(first_away, "dp", swap)
    right_here = right_send(right_rows)
    mark = run_forward(0, 0, mark)
    mark = run_add((0, 0), mark, right_here)
    mark = run_forward(0, 1, mark)
    right_there = lax.ppermute(right_here, "dp", swap)
    mark = run_half(1, mark)
    right_own, for_other, mark = right_products(
        features, right_rows, right_here, right_there, where, [mark]
    )
    received = lax.ppermute(for_other, ("tensor", "query"), back)
    mark = run_add((0, 1), mark, theirs[0, 0], received)
    mark = run_slope((0, 0), mark)
    mark = run_forward(1, 0, mark)
    right_part, mark = right_choice(right_own, received, owns, [mark])
    right_other = across(right_part, 1)
    mark = run_add((1, 0), mark)
    mark = run_forward(1, 1, mark)
    mark = run_slope((0, 1), mark)
    mark = run_add((1, 1), mark)
    mark = run_backward((0, 0), False, mark)
    right_sum = right_part
    for step in range(1, tensor_size.bit_length() - 1):
        right_sum, message, mark = add_right(right_sum, right_other, [mark])
        right_other = across(message, 1 << step)
    mark = run_backward((0, 1), True, mark, *adds[2, 0][1])
    send_sums(0)
    mark = run_slope((1, 0), mark, right_other)
    mark = run_backward((1, 0), False, mark)
    mark = run_add((2, 0), mark)
    mark = run_slope((1, 1), mark, arrived[0][0])
    mark = run_backward((1, 1), True, mark)
    send_sums(1)
    mark = run_add((2, 1), mark)
    mark = add_sums(0, mark)
    mark = run_slope((2, 0), mark)
    mark = run_backward((2, 0), False, mark)
    mark = run_slope((2, 1), mark, arrived[1][0])
    mark = run_backward((2, 1), True, mark)
    send_sums(2)
    mark = add_sums(1, mark)
    mark = add_sums(2, mark)

    right_sum = right_sum.astype(F32) + right_other.astype(F32)
    weighted, grads = 0.0, []
    for t, (low, high) in enumerate(tokens):
        membership = (
            token_ids[None, low:high] == jnp.arange(EXAMPLES, dtype=jnp.int32)[:, None]
        ).astype(F32)
        weighted = weighted + exact_dot(membership, lefts[t] * right_sum[low:high])
        grads.append(results[t])
    choice = column_choice(query_ids, query_count, rank_count)
    scores = lax.psum(exact_dot(weighted, choice) / rank_count, ("tensor", "dp"))
    return jnp.concatenate(grads, axis=0), scores


def broadcast(value, axis, source):
    kept = jnp.where(lax.axis_index(axis) == source, value, 0).astype(value.dtype)
    return lax.psum(kept, axis)


def general(features, up_weight, out_grad, left_factors, right_factors, token_ids, query_ids):
    query_count, rank_count = left_factors.shape[:2]
    local_rows = lax.all_gather(up_weight, "dp", axis=0, tiled=True)
    preact_part = jnp.dot(features, local_rows, preferred_element_type=jnp.float32)
    preact_share = lax.psum_scatter(preact_part, "query", scatter_dimension=0, tiled=True)
    share_rows = preact_share.shape[0]
    own_grad = lax.dynamic_slice_in_dim(
        out_grad, lax.axis_index("query") * share_rows, share_rows, 0
    )
    grad_rows = lax.all_gather(silu_slope(preact_share, own_grad), "query", axis=0, tiled=True)
    input_part = contract_last(grad_rows, local_rows)
    input_grad = lax.psum_scatter(input_part, "tensor", scatter_dimension=1, tiled=True).astype(
        jnp.bfloat16
    )
    fold_ratio = lax.axis_size("tensor") // lax.axis_size("query")
    tensor_index = lax.axis_index("tensor")
    block_width = right_factors.shape[2]
    feature_piece = lax.dynamic_slice_in_dim(
        features, tensor_index % fold_ratio * block_width, block_width, 1
    )
    feature_block = broadcast(feature_piece, "query", tensor_index // fold_ratio)
    left_proj = contract_last(
        grad_rows, left_factors.reshape(query_count * rank_count, left_factors.shape[2])
    )
    right_proj = contract_last(
        feature_block, right_factors.reshape(query_count * rank_count, block_width)
    )
    left_sum, right_sum = lax.psum((left_proj, right_proj), "tensor")
    membership = (token_ids[None, :] == jnp.arange(EXAMPLES, dtype=jnp.int32)[:, None]).astype(
        jnp.float32
    )
    weighted = exact_dot(membership, left_sum * right_sum)
    choice = column_choice(query_ids, query_count, rank_count)
    scores = lax.psum(exact_dot(weighted, choice) / rank_count, "dp")
    return (input_grad, scores)


def solution(mesh):
    size = mesh.shape
    is_paired = size["query"] == 2 and size["dp"] == 2 and size["tensor"] in (2, 4, 8, 16)
    return jax.shard_map(
        paired if is_paired else general,
        mesh=mesh,
        in_specs=(
            P(("groups", "dp"), "query"),
            P(("query", "dp"), "tensor"),
            P(("groups", "dp"), "tensor"),
            P("query", None, "tensor"),
            P("query", None, "tensor"),
            P(("groups", "dp")),
            P("query", None),
        ),
        out_specs=(P(("groups", "dp"), ("query", "tensor")), P("groups", "query")),
        check_vma=False,
    )
```
